512 devices in a mesh: corpus: 64 (over x, y, core), tensor: 8 (over z).
Axes of the slice: x: 4, y: 8, z: 8, core: 2. Of those that a mesh axis runs over, the one named last changes fastest.
Arguments:
- self_query: bfloat16 [1024, 4, 4096], P('corpus', None, 'tensor'), may hold values from -24 to 24
- cross_query: bfloat16 [1024, 4, 4096], P('corpus', None, 'tensor'), may hold values from -24 to 24
- cache: bfloat16 [1024, 2, 64, 4096], P('corpus', None, None, 'tensor'), may hold values from -24 to 24
- step_kv: bfloat16 [1024, 2, 4, 4096], P('corpus', None, None, 'tensor'), may hold values from -6 to 6
- kv_length: int32 [1024], P('corpus'), may hold values from 2 to 64
- positions: int32 [1024], P('corpus'), may hold values from 125 to 4095, as said below
- corpus_kv: bfloat16 [512, 2, 128, 4096], P('corpus', None, None, 'tensor'), may hold values from -24 to 24
- neighbour_shard: int32 [1024, 4], P('corpus'), may hold values from 0 to 63, all different within a row; in each aligned block of 16 rows (0 to 15, 16 to 31, ...) at most 2 rows name the same one
- neighbour_slot: int32 [1024, 4], P('corpus'), may hold values from 0 to 7
- out_weight: bfloat16 [4096, 8192], P('tensor', 'corpus'), may hold values from -0.09375 to 0.09375
Outputs:
- self_heads: bfloat16 [1024, 4, 4096], P('corpus', None, 'tensor')
- cross_out: bfloat16 [64, 64, 8192], P('tensor', None, 'corpus')
The draws below stay inside these ranges and needn't reach their ends.
Inputs may be any that keep to these rules, and one draw needn't show every extreme that they name: `neighbour_shard`: the (4) shards of one request are distinct; the first 2 serve the span in progress, the others the next span. Among the requests of one replica (aligned blocks of 16 requests) no shard is named more than 2 times, a bound that some block reaches. Each first decoded position lies 1 to 3 positions before a multiple of 64.
All inputs are finite; a program needn't handle non-finite values.
Results may differ from the reference program's by a relative error of at most 0.0055.
Values may be sent and summed in bfloat16 or wider, within the bound.
A program may use at most 64 MiB of HBM per device.

```python
import math
import jax
import jax.numpy as jnp
import numpy as np
from jax import lax

D = 8192
HDIM = 128
HEADS = 32
NTOK = 128
NBR = 2
SPAN = 64
STEPS = 4
BLK_DEV = 8
REQ_DEV = 16
LMAX = 64
CAP = 2
REQUESTS = 1024
BLOCKS = 512
N_CORPUS = 64


def drawn_queries(key):
    base_key = jax.random.fold_in(key, 0)
    shape = (REQUESTS, STEPS, HEADS * HDIM)
    values = jax.random.normal(base_key, shape, jnp.float32)
    return values.astype(jnp.bfloat16)


def drawn_states(key, count, length):
    shape = (count, 2, length, HEADS * HDIM)
    values = jax.random.normal(key, shape, jnp.float32)
    return values.astype(jnp.bfloat16)


def draw_self_query(key, part):
    key = jax.random.fold_in(key, 11)
    return drawn_queries(key)


def draw_cross_query(key, part):
    key = jax.random.fold_in(key, 12)
    return drawn_queries(key)


def draw_cache(key, part):
    key = jax.random.fold_in(key, 13)
    return drawn_states(key, REQUESTS, LMAX)


def draw_corpus_kv(key, part):
    key = jax.random.fold_in(key, 14)
    return drawn_states(key, BLOCKS, NTOK)


def draw_kv_length(key, part):
    key = jax.random.fold_in(key, 15)
    lengths = jax.random.randint(key, (REQUESTS,), 2, LMAX + 1)
    lengths = lengths.at[0].set(LMAX)
    return lengths.at[REQUESTS - 1].set(2).astype(jnp.int32)


def draw_positions(key, part):
    key = jax.random.fold_in(key, 16)
    first_key, second_key = jax.random.split(key)
    span_index = jax.random.randint(first_key, (REQUESTS,), 1, 64)
    before = jax.random.randint(second_key, (REQUESTS,), 1, 4)
    values = span_index * SPAN + SPAN - before
    values = values.at[0].set(64 * SPAN - 1)
    return values.at[REQUESTS - 1].set(2 * SPAN - 3).astype(jnp.int32)


def with_ends(drawn, rng, low, top_value):
    longest = drawn.shape.index(max(drawn.shape))
    spots = []
    for shift in (0, 1):
        where = [jax.random.randint(jax.random.fold_in(rng, axis), (), 0, length) for axis, length in enumerate(drawn.shape)]
        where[longest] = (where[longest] + shift) % drawn.shape[longest]
        spots.append(tuple(where))
    return drawn.at[spots[0]].set(low).at[spots[1]].set(top_value)


def level_of(rng, shape, cuts, low, largest):
    loudness, own = 1.0, jax.random.fold_in(rng, 6)
    for dim, parts in cuts:
        draws = jnp.exp(jax.random.uniform(jax.random.fold_in(own, dim), (parts,), jnp.float32, low / len(cuts), largest / len(cuts)))
        loudness = loudness * jnp.repeat(draws, shape[dim] // parts).reshape([-1 if axis == dim else 1 for axis in range(len(shape))])
    return loudness


def assign_block(rng, own, number, rows, count, top, most, skew):
    order = jax.random.permutation(rng, count)
    crowded, ordinary = load_shares(count, rows * top, most, skew, True), load_shares(count, rows * top, most, skew, False)
    places = jnp.arange(count)

    def named(sizes, turn):
        used = int((sizes > 0).sum())
        fixed = max(1, used // 4)
        moved = fixed + (places - fixed + turn * (used - fixed)) % max(1, count - fixed)
        return jnp.zeros((count,), jnp.int32).at[order[jnp.where(places < fixed, places, moved)]].set(jnp.asarray(sizes, jnp.int32))

    sizes = jnp.where(number % 4 == 0, named(crowded, number // 4), named(ordinary, number - number // 4 - 1))
    mixed = jax.random.permutation(jax.random.fold_in(own, 3), count)
    source_of, receiver = mixed[0:count // 2 * 2:2], mixed[1:count // 2 * 2:2]
    slack = jnp.minimum(sizes[source_of] - 1, most - sizes[receiver]) // 2
    slack = jnp.where((source_of == order[0]) | (receiver == order[0]) | (sizes[receiver] == 0), 0, jnp.maximum(slack, 0))
    moved = jax.random.randint(jax.random.fold_in(own, 4), (count // 2,), 0, 1 << 20) % (slack + 1)
    sizes = sizes.at[source_of].add(-moved).at[receiver].add(moved)
    items = jnp.searchsorted(jnp.cumsum(sizes), jnp.arange(rows * top), side="right").astype(jnp.int32)
    listing = items.reshape(top, rows).T
    listing = listing[jax.random.permutation(jax.random.fold_in(own, 1), rows)]
    turn = jax.random.randint(jax.random.fold_in(own, 2), (rows, 1), 0, top)
    return jnp.take_along_axis(listing, (jnp.arange(top)[None, :] + turn) % top, axis=1)


def load_shares(count, total, limit, lean, full):
    weights = [(1 << 20) // math.isqrt(rank ** lean) + 1 for rank in range(1, count + 1)]
    largest = limit if full else min(limit, max(-(-total // count), total * weights[0] // sum(weights)))
    least = 1 if total - largest >= count - 1 else 0
    counts, rest = [largest] + [least] * (count - 1), total - largest - least * (count - 1)
    while rest > 0:
        candidates = [i for i in range(1, count) if counts[i] < largest] or [i for i in range(1, count) if counts[i] < limit]
        whole, budget = sum([weights[i] for i in candidates]), rest
        for i in candidates:
            extra = min(limit - counts[i], max(1, budget * weights[i] // whole), rest)
            counts[i] = counts[i] + extra
            rest = rest - extra
    return np.array(counts)


def centred(key, shape, deviation, reach, pieces=(), held_as=jnp.bfloat16):
    gain = level_of(key, shape, pieces, -0.22, 0.18) if pieces else 1.0
    array = jax.random.normal(key, shape, jnp.float32) * deviation * gain
    return jnp.minimum(jnp.maximum(array, -reach), reach).astype(held_as)


def setup_inputs(seed: int = 0) -> dict:
    streams_of = jax.random.split(jax.random.key(seed), 11)
    self_query = draw_self_query(jax.random.fold_in(streams_of[10], 71), 0)
    cross_query = draw_cross_query(jax.random.fold_in(streams_of[10], 71), 0)
    cache = draw_cache(jax.random.fold_in(streams_of[10], 71), 0)
    step_kv = centred(streams_of[3], (REQUESTS, 2, STEPS, HEADS * HDIM), 1.0, 6.0, ((0, 64), (3, 8)))
    kv_length = draw_kv_length(jax.random.fold_in(streams_of[10], 71), 0)
    positions = draw_positions(jax.random.fold_in(streams_of[10], 71), 0)
    corpus_kv = draw_corpus_kv(jax.random.fold_in(streams_of[10], 71), 0)
    neighbour_shard_keys = jax.random.split(jax.random.fold_in(streams_of[7], 1), REQUESTS // REQ_DEV)
    neighbour_shard_turns = jax.random.permutation(jax.random.fold_in(streams_of[7], 3), REQUESTS // REQ_DEV)
    neighbour_shard = jax.vmap(lambda own, number: assign_block(jax.random.fold_in(streams_of[7], 2), own, number, REQ_DEV, N_CORPUS, 2 * NBR, CAP, 2))(neighbour_shard_keys, neighbour_shard_turns).reshape((REQUESTS, 2 * NBR))
    neighbour_slot = with_ends(jax.random.randint(streams_of[8], (REQUESTS, 2 * NBR), 0, BLK_DEV), jax.random.fold_in(streams_of[8], 1), 0, BLK_DEV - 1).astype(jnp.int32)
    out_weight = centred(streams_of[9], (HEADS * HDIM, D), (HEADS * HDIM) ** -0.5, 0.09375, ((0, 8), (1, 64)))
    return dict(self_query=self_query, cross_query=cross_query, cache=cache, step_kv=step_kv, kv_length=kv_length, positions=positions, corpus_kv=corpus_kv, neighbour_shard=neighbour_shard, neighbour_slot=neighbour_slot, out_weight=out_weight)


masked_value = -1e30


def attend_request(queries, cached, fresh, length):
    step_count = queries.shape[0]
    head_count = queries.shape[1] // HDIM
    score_scale = HDIM ** -0.5
    query_heads = queries.astype(jnp.float32).reshape(step_count, head_count, HDIM)
    cache_keys = cached[0].astype(jnp.float32).reshape(-1, head_count, HDIM)
    cache_values = cached[1].astype(jnp.float32).reshape(-1, head_count, HDIM)
    fresh_keys = fresh[0].astype(jnp.float32).reshape(step_count, head_count, HDIM)
    fresh_values = fresh[1].astype(jnp.float32).reshape(step_count, head_count, HDIM)
    cache_scores = jnp.einsum("thd,lhd->thl", query_heads, cache_keys) * score_scale
    is_live = jnp.arange(cache_keys.shape[0], dtype=jnp.int32) < length
    cache_scores = jnp.where(is_live[None, None, :], cache_scores, masked_value)
    fresh_scores = jnp.einsum("thd,uhd->thu", query_heads, fresh_keys) * score_scale
    causal = jnp.arange(step_count)[None, :] <= jnp.arange(step_count)[:, None]
    fresh_scores = jnp.where(causal[:, None, :], fresh_scores, masked_value)
    row_max = jnp.maximum(jnp.max(cache_scores, axis=-1), jnp.max(fresh_scores, axis=-1))
    cache_exp = jnp.exp(cache_scores - row_max[..., None])
    fresh_exp = jnp.exp(fresh_scores - row_max[..., None])
    totals = jnp.sum(cache_exp, axis=-1) + jnp.sum(fresh_exp, axis=-1)
    cache_low = lax.optimization_barrier(cache_exp.astype(jnp.bfloat16)).astype(jnp.float32)
    fresh_low = lax.optimization_barrier(fresh_exp.astype(jnp.bfloat16)).astype(jnp.float32)
    weighted = jnp.einsum("thl,lhd->thd", cache_low, cache_values)
    weighted = weighted + jnp.einsum("thu,uhd->thd", fresh_low, fresh_values)
    return (weighted / totals[..., None]).astype(jnp.bfloat16).reshape(step_count, -1)


def cross_request(queries, shards, slots, position, corpus_kv):
    step_count = queries.shape[0]
    head_count = queries.shape[1] // HDIM
    score_scale = HDIM ** -0.5
    query_heads = queries.astype(jnp.float32).reshape(step_count, head_count, HDIM)
    block_ids = (shards * BLK_DEV + slots).astype(jnp.int32)
    blocks = corpus_kv[block_ids].astype(jnp.float32)
    item_count = blocks.shape[0]
    block_keys = blocks[:, 0].reshape(item_count, -1, head_count, HDIM)
    block_values = blocks[:, 1].reshape(item_count, -1, head_count, HDIM)
    item_scores = jnp.einsum("thd,pnhd->pthn", query_heads, block_keys) * score_scale
    item_max = jnp.max(item_scores, axis=-1)
    item_exp = jnp.exp(item_scores - item_max[..., None])
    item_total = jnp.sum(item_exp, axis=-1)
    item_low = lax.optimization_barrier(item_exp.astype(jnp.bfloat16)).astype(jnp.float32)
    item_sums = jnp.einsum("pthn,pnhd->pthd", item_low, block_values)
    boundary = SPAN - position % SPAN
    use_next = jnp.arange(step_count, dtype=jnp.int32) >= boundary
    chosen_sums = jnp.where(use_next[None, :, None, None], item_sums[NBR:], item_sums[:NBR])
    chosen_max = jnp.where(use_next[None, :, None], item_max[NBR:], item_max[:NBR])
    chosen_total = jnp.where(use_next[None, :, None], item_total[NBR:], item_total[:NBR])
    joint = jnp.max(chosen_max, axis=0)
    factors = jnp.exp(chosen_max - joint[None])
    numer = jnp.sum(factors[..., None] * chosen_sums, axis=0)
    denom = jnp.sum(factors * chosen_total, axis=0)
    return (numer / denom[..., None]).astype(jnp.bfloat16).reshape(step_count, -1)


def reference(self_query, cross_query, cache, step_kv, kv_length, positions, corpus_kv, neighbour_shard, neighbour_slot, out_weight):
    def self_one(packed):
        return attend_request(packed[0], packed[1], packed[2], packed[3])

    def cross_one(packed):
        return cross_request(packed[0], packed[1], packed[2], packed[3], corpus_kv)

    self_heads = lax.map(self_one, (self_query, cache, step_kv, kv_length))
    cross_heads = lax.map(cross_one, (cross_query, neighbour_shard, neighbour_slot, positions))
    flat_heads = cross_heads.reshape(-1, cross_heads.shape[-1])
    projected = jnp.dot(flat_heads, out_weight, preferred_element_type=jnp.float32).astype(jnp.bfloat16)
    cross_out = projected.reshape(N_CORPUS, -1, projected.shape[-1]).transpose(1, 0, 2)
    return self_heads, cross_out
```

```python
import functools

import jax
import jax.numpy as jnp
from jax import lax
from jax.experimental import pallas as pl
from jax.experimental.pallas import tpu as pltpu
from jax.sharding import PartitionSpec as P

HDIM = 128
NBR = 2
SPAN = 64
CORES = 2
GRID_OF = {64: (4, 8), 8: (2, 2)}
MESH = pl.DeviceIdType.MESH
masked_value = -1e30
F32 = jnp.float32
BF16 = jnp.bfloat16


def pack_kernel(shard_ref, slot_ref, query_ref, send_ref, rank_ref, base, variants, total, counts):
    request_count, step_count, _ = query_ref.shape
    shard_count, message_rows, _ = send_ref.shape
    head_count = message_rows // 8
    base[...] = jnp.zeros_like(base)
    queries = query_ref[...].astype(F32)
    for head in range(head_count):
        base[:, head * 8 : head * 8 + step_count, :] = queries[:, :, head * HDIM : (head + 1) * HDIM]
    flat = base[...].reshape(request_count * message_rows, HDIM)
    row = lax.broadcasted_iota(jnp.int32, flat.shape, 0) % 8
    size = flat.shape[0]
    moved = (
        jnp.where(row < 3, flat, 0.0),
        jnp.where((row >= 3) & (row < 6), pltpu.roll(flat, 3, 0), 0.0),
        jnp.where(row < 3, pltpu.roll(flat, size - 1, 0), 0.0),
        jnp.where((row >= 3) & (row < 6), pltpu.roll(flat, 2, 0), 0.0),
    )
    for number, values in enumerate(moved):
        variants[number] = values.reshape(request_count, message_rows, HDIM)
    total[...] = jnp.zeros_like(total)

    def clear(index, carry):
        counts[index] = 0
        return carry

    lax.fori_loop(0, shard_count, clear, 0)
    tile_row = lax.broadcasted_iota(jnp.int32, (message_rows, HDIM), 0) % 8

    def place(request, carry):
        for item in range(2 * NBR):
            shard = shard_ref[request, item]
            rank = counts[shard]
            counts[shard] = rank + 1
            rank_ref[request, item] = rank
            number = rank + (2 if item >= NBR else 0)
            tag = (slot_ref[request, item] + 1).astype(F32)
            tile = jnp.where(tile_row == rank + 6, tag, variants[number, request])
            total[shard] = total[shard] + tile
        return carry

    lax.fori_loop(0, request_count, place, 0)
    send_ref[...] = total[...].astype(BF16)


def attend_self(query_ref, fresh_ref, cached, length_ref, out_ref):
    request_count, _, cache_length, _ = cached.shape
    row_count, width = query_ref.shape
    step_count = row_count // request_count
    key_count = request_count * cache_length
    row_request = lax.broadcasted_iota(jnp.int32, (row_count, key_count), 0) // step_count
    key_index = lax.broadcasted_iota(jnp.int32, (1, key_count), 1)
    limit = jnp.zeros((1, key_count), jnp.int32)
    for request in range(request_count):
        limit = jnp.where(key_index // cache_length == request, length_ref[request], limit)
    key_request = jnp.where(key_index % cache_length < limit, key_index // cache_length, -1)
    live = row_request == key_request
    fresh_row = lax.broadcasted_iota(jnp.int32, (row_count, row_count), 0)
    fresh_key = lax.broadcasted_iota(jnp.int32, (row_count, row_count), 1)
    fresh_live = (fresh_row // step_count == fresh_key // step_count) & (fresh_key <= fresh_row)
    scale = HDIM ** (-0.5)
    last = (((1,), (1,)), ((), ()))
    for head in range(width // HDIM):
        lanes = slice(head * HDIM, (head + 1) * HDIM)
        query = query_ref[:, lanes]
        keys = cached[:, 0, :, lanes].reshape(key_count, HDIM)
        values = cached[:, 1, :, lanes].reshape(key_count, HDIM)
        scores = lax.dot_general(query, keys, last, preferred_element_type=F32) * scale
        scores = jnp.where(live, scores, masked_value)
        fresh = lax.dot_general(query, fresh_ref[0, :, lanes], last, preferred_element_type=F32) * scale
        fresh = jnp.where(fresh_live, fresh, masked_value)
        top = jnp.maximum(
            jnp.max(scores, axis=1, keepdims=True), jnp.max(fresh, axis=1, keepdims=True)
        )
        weights = jnp.exp(scores - top)
        fresh_weights = jnp.exp(fresh - top)
        denom = jnp.sum(weights, axis=1, keepdims=True) + jnp.sum(fresh_weights, axis=1, keepdims=True)
        summed = jnp.dot(weights.astype(BF16), values, preferred_element_type=F32)
        summed = summed + jnp.dot(
            fresh_weights.astype(BF16), fresh_ref[1, :, lanes], preferred_element_type=F32
        )
        out_ref[:, lanes] = (summed / denom).astype(BF16)


def attend_blocks(messages, blocks):
    source_count, message_rows, _ = messages.shape
    head_count = message_rows // 8
    block_count, _, token_count, _ = blocks.shape
    rows = source_count * 8
    scale = HDIM ** (-0.5)
    values = messages.astype(F32)
    in_tile = lax.broadcasted_iota(jnp.int32, (source_count, 8, HDIM), 1)
    lane = lax.broadcasted_iota(jnp.int32, (source_count, 8, HDIM), 2)
    tags = jnp.where(in_tile < 3, values[:, 6:7, :], values[:, 7:8, :]).reshape(rows, HDIM)
    mine = [tags == F32(index + 1) for index in range(block_count)]
    parts = []
    for head in range(head_count):
        lanes = slice(head * HDIM, (head + 1) * HDIM)
        query = values[:, head * 8 : head * 8 + 8, :].reshape(rows, HDIM).astype(BF16)
        keys = blocks[:, 0, :, lanes].reshape(block_count * token_count, HDIM)
        scores = lax.dot_general(
            query, keys, (((1,), (1,)), ((), ())), preferred_element_type=F32
        )
        chosen = jnp.zeros((rows, token_count), F32)
        for index in range(block_count):
            chosen = jnp.where(
                mine[index], scores[:, index * token_count : (index + 1) * token_count], chosen
            )
        chosen = chosen * scale
        top = jnp.max(chosen, axis=1, keepdims=True)
        weights = jnp.exp(chosen - top)
        denom = jnp.sum(weights, axis=1, keepdims=True)
        spread = jnp.concatenate(
            [jnp.where(mine[index], weights, 0.0).astype(BF16) for index in range(block_count)], axis=1
        )
        held = blocks[:, 1, :, lanes].reshape(block_count * token_count, HDIM)
        summed = jnp.dot(spread, held, preferred_element_type=F32) / denom
        level = jnp.broadcast_to(top + jnp.log(denom), (rows, HDIM)).reshape(source_count, 8, HDIM)
        level = jnp.sum(jnp.where(lane % 8 == in_tile, level, 0.0), axis=1, keepdims=True)
        high = level.astype(BF16).astype(F32)
        middle = (level - high).astype(BF16).astype(F32)
        low = level - high - middle
        terms = jnp.where(lane < 8, high, jnp.where(lane < 16, middle, low))
        parts.append(jnp.where(in_tile == 6, terms, summed.reshape(source_count, 8, HDIM)))
    return jnp.concatenate(parts, axis=1).astype(BF16)


def row_levels(values):
    source_count, message_rows, _ = values.shape
    tiles = values.reshape(source_count * message_rows // 8, 8, HDIM)
    in_tile = lax.broadcasted_iota(jnp.int32, tiles.shape, 1)
    lane = lax.broadcasted_iota(jnp.int32, tiles.shape, 2)
    terms = jnp.broadcast_to(tiles[:, 6:7, :], tiles.shape)
    picked = jnp.where((lane < 24) & (lane % 8 == in_tile), terms, 0.0)
    levels = jnp.sum(picked, axis=2, keepdims=True)
    return jnp.broadcast_to(levels, tiles.shape).reshape(values.shape)


def main_kernel(
    shard_ref, rank_ref, position_ref, length_ref,
    send_ref, query_ref, fresh_ref, cache_ref, corpus_ref, weight_ref,
    self_ref, out_ref,
    cached, blocks, arrived, reply, returned, sums, levels,
    heads, gathered, weights, totals, out_send, out_recv,
    local_sem, query_send, query_recv, reply_send, reply_recv,
    x_send, x_recv, ring_send, ring_recv, head_send, head_recv,
    y_send, y_recv, core_send, core_recv, out_send_sem, out_recv_sem,
):
    shard_count, message_rows, _ = send_ref.shape
    x_count, y_count = GRID_OF[shard_count]
    layer = y_count * CORES
    tensor_count = gathered.shape[1]
    request_count = shard_ref.shape[0]
    me, mine = lax.axis_index("corpus"), lax.axis_index("tensor")
    x = me // layer
    y = (me // CORES) % y_count
    core = me % CORES

    def device_at(dx, dy, dc):
        return (((x + dx) % x_count) * y_count + (y + dy) % y_count) * CORES + (core + dc) % CORES

    def remote(source, target, send_sem, recv_sem, corpus=None, tensor=None):
        return pltpu.make_async_remote_copy(
            src_ref=source,
            dst_ref=target,
            send_sem=send_sem,
            recv_sem=recv_sem,
            device_id=(me if corpus is None else corpus, mine if tensor is None else tensor),
            device_id_type=MESH,
        )

    def wait_bytes(ref, sem):
        pltpu.make_async_copy(ref, ref, sem).wait()

    barrier = pltpu.get_barrier_semaphore()

    def greet_corpus(step, carry):
        pl.semaphore_signal(
            barrier, inc=1, device_id=((me + step) % shard_count, mine), device_id_type=MESH
        )
        return carry

    def greet_tensor(step, carry):
        pl.semaphore_signal(
            barrier, inc=1, device_id=(me, (mine + step) % tensor_count), device_id_type=MESH
        )
        return carry

    lax.fori_loop(1, shard_count, greet_corpus, 0)
    lax.fori_loop(1, tensor_count, greet_tensor, 0)
    cache_copy = pltpu.make_async_copy(cache_ref, cached, local_sem.at[0])
    corpus_copy = pltpu.make_async_copy(corpus_ref, blocks, local_sem.at[1])
    cache_copy.start()
    corpus_copy.start()
    columns = pl.ds(pl.multiple_of(x * HDIM, HDIM), HDIM)
    own_weight = pltpu.make_async_copy(weight_ref, weights.at[mine, :, columns], local_sem.at[2])
    own_weight.start()
    own_query = pltpu.make_async_copy(send_ref.at[me], arrived.at[me], query_recv.at[0])
    own_query.start()
    pl.semaphore_wait(barrier, shard_count - 1 + tensor_count - 1)

    def send_query(step, carry):
        target = device_at(step // layer, (step % layer) // CORES, step % CORES)
        remote(
            send_ref.at[target], arrived.at[me], query_send, query_recv.at[step // layer], target
        ).start()
        return carry

    lax.fori_loop(1, shard_count, send_query, 0)
    for dx in range(1, x_count):
        remote(
            weight_ref, weights.at[mine, :, columns], x_send, x_recv, device_at(dx, 0, 0)
        ).start()

    def ring_up(step):
        owner = (mine - step + tensor_count) % tensor_count
        return remote(
            weights.at[owner], weights.at[owner], ring_send.at[0, step], ring_recv.at[0, step],
            tensor=(mine + 1) % tensor_count,
        )

    def ring_down(step):
        owner = (mine + step) % tensor_count
        return remote(
            weights.at[owner], weights.at[owner], ring_send.at[1, step], ring_recv.at[1, step],
            tensor=(mine + tensor_count - 1) % tensor_count,
        )

    ups, downs = tensor_count // 2, (tensor_count - 1) // 2

    def ring_wait(step):
        if 0 <= step < ups:
            ring_up(step).wait_recv()
        if 0 <= step < downs:
            ring_down(step).wait_recv()

    def ring_step(step):
        ring_wait(step - 1)
        if step < ups:
            ring_up(step).start()
        if step < downs:
            ring_down(step).start()

    cache_copy.wait()
    attend_self(query_ref, fresh_ref, cached, length_ref, self_ref)

    own_weight.wait()
    x_wait = weights.at[mine, :, pl.ds(0, (x_count - 1) * HDIM)]
    wait_bytes(x_wait, x_recv)
    ring_step(0)

    corpus_copy.wait()

    def serve(dx, carry):
        first = pl.multiple_of(((x - dx + x_count) % x_count) * layer, layer)
        chunk = pl.ds(first, layer)
        wait_bytes(arrived.at[chunk], query_recv.at[dx])
        reply[chunk] = attend_blocks(arrived[chunk], blocks)

        def answer(step, inner):
            target = device_at(x_count - dx, step // CORES, step % CORES)
            remote(
                reply.at[target], returned.at[me], reply_send, reply_recv.at[dx], target
            ).start()
            return inner

        lax.fori_loop(jnp.where(dx == 0, 1, 0), layer, answer, 0)
        return carry

    lax.fori_loop(0, x_count, serve, 0)
    own_reply = pltpu.make_async_copy(reply.at[me], returned.at[me], reply_recv.at[0])
    own_reply.start()
    ring_step(1)

    def decode(dx, carry):
        first = pl.multiple_of(((x + dx) % x_count) * layer, layer)
        chunk = pl.ds(first, layer)
        wait_bytes(returned.at[chunk], reply_recv.at[dx])
        values = returned[chunk].astype(F32)
        sums[chunk] = values
        levels[chunk] = row_levels(values)
        return carry

    lax.fori_loop(0, x_count, decode, 0)

    tile_row = lax.broadcasted_iota(jnp.int32, (message_rows, HDIM), 0) % 8

    def combined(request):
        boundary = SPAN - position_ref[request] % SPAN
        late = tile_row >= boundary

        def item(ref, number):
            tile = ref[shard_ref[request, number]]
            second = rank_ref[request, number] == 1
            if number < NBR:
                return jnp.where(second, pltpu.roll(tile, message_rows - 3, 0), tile)
            return jnp.where(
                second, pltpu.roll(tile, message_rows - 2, 0), pltpu.roll(tile, 1, 0)
            )

        def pair(ref):
            return [
                jnp.where(late, item(ref, NBR + number), item(ref, number)) for number in range(NBR)
            ]

        held, level = pair(sums), pair(levels)
        joint = jnp.maximum(level[0], level[1])
        factors = [jnp.exp(entry - joint) for entry in level]
        return (factors[0] * held[0] + factors[1] * held[1]) / (factors[0] + factors[1])

    def combine(owner, carry):
        first = combined(owner * 2)
        second = pltpu.roll(combined(owner * 2 + 1), 4, 0)
        both = jnp.where(tile_row < 4, first, second)
        upper = jnp.concatenate([both[0:8], both[8:16]], axis=1)
        lower = jnp.concatenate([both[16:24], both[24:32]], axis=1)
        heads[owner] = jnp.concatenate([upper, lower], axis=0).astype(BF16)
        return carry

    lax.fori_loop(0, tensor_count, combine, 0)

    place = y * CORES + core
    own_heads = pltpu.make_async_copy(heads.at[mine], gathered.at[place, mine], head_recv)
    own_heads.start()

    def send_heads(step, carry):
        owner = (mine + step) % tensor_count
        remote(
            heads.at[owner], gathered.at[place, mine], head_send, head_recv, tensor=owner
        ).start()
        return carry

    lax.fori_loop(1, tensor_count, send_heads, 0)
    ring_step(2)
    wait_bytes(gathered.at[place], head_recv)

    def send_y(step, carry):
        remote(
            gathered.at[place], gathered.at[place], y_send, y_recv.at[step], device_at(0, step, 0)
        ).start()
        return carry

    def pass_core(index):
        return remote(
            gathered.at[index], gathered.at[index], core_send, core_recv, device_at(0, 0, 1)
        )

    lax.fori_loop(1, y_count, send_y, 0)
    pass_core(place).start()
    ring_step(3)

    def forward(step, carry):
        index = ((y - step + y_count) % y_count) * CORES + core
        wait_bytes(gathered.at[index], y_recv.at[step])
        pass_core(index).start()
        return carry

    lax.fori_loop(1, y_count, forward, 0)
    ring_wait(3)
    wait_bytes(gathered.at[pl.ds(0, y_count)], core_recv)

    half = gathered.shape[2] // 2
    rows = layer * half

    def project(owner):
        block = gathered[:, owner].astype(F32)
        left = jnp.concatenate(
            [block[:, :half].reshape(rows, -1), block[:, half:].reshape(rows, -1)], axis=1
        ).astype(BF16)
        return jnp.dot(left, weights[owner], preferred_element_type=F32)

    totals[...] = jnp.zeros_like(totals)

    def accumulate(owner, carry):
        product = project(owner)
        for dx in range(x_count):
            totals[dx * rows : (dx + 1) * rows, :] += product[:, dx * HDIM : (dx + 1) * HDIM]
        return carry

    lax.fori_loop(0, tensor_count, accumulate, 0)
    for row in range(half):
        for index in range(x_count):
            picked = totals[pl.ds(index * rows + row, layer, stride=half), :]
            out_send[index, row] = picked.astype(BF16)
    own_out = pltpu.make_async_copy(out_send.at[x], out_recv.at[x], out_recv_sem)
    own_out.start()
    for dx in range(1, x_count):
        remote(
            out_send.at[(x + dx) % x_count], out_recv.at[x], out_send_sem, out_recv_sem,
            device_at(dx, 0, 0),
        ).start()
    wait_bytes(out_recv, out_recv_sem)
    for index in range(x_count):
        out_ref[:, index * layer : (index + 1) * layer, :] = out_recv[index]

    wait_bytes(send_ref.at[pl.ds(0, shard_count - 1)], query_send)
    wait_bytes(reply.at[pl.ds(0, shard_count - 1)], reply_send)
    wait_bytes(x_wait, x_send)
    for step in range(ups):
        ring_up(step).wait_send()
    for step in range(downs):
        ring_down(step).wait_send()
    wait_bytes(heads.at[pl.ds(0, tensor_count - 1)], head_send)
    wait_bytes(gathered.at[pl.ds(0, y_count - 1)], y_send)
    wait_bytes(gathered.at[pl.ds(0, y_count)], core_send)
    wait_bytes(out_send.at[pl.ds(0, x_count - 1)], out_send_sem)


def on_device(
    self_query,
    cross_query,
    cache,
    step_kv,
    kv_length,
    positions,
    corpus_kv,
    neighbour_shard,
    neighbour_slot,
    out_weight,
):
    request_count, step_count, width = cross_query.shape
    head_count = width // HDIM
    shard_count = lax.axis_size("corpus")
    tensor_count = lax.axis_size("tensor")
    x_count, y_count = GRID_OF[shard_count]
    layer = y_count * CORES
    message_rows = head_count * 8
    row_count = request_count * step_count
    share = row_count // tensor_count
    smem = pl.BlockSpec(memory_space=pltpu.SMEM)
    vmem = pl.BlockSpec(memory_space=pltpu.VMEM)
    message = (shard_count, message_rows, HDIM)
    send, ranks = pl.pallas_call(
        pack_kernel,
        out_shape=(
            jax.ShapeDtypeStruct(message, BF16),
            jax.ShapeDtypeStruct(neighbour_shard.shape, jnp.int32),
        ),
        in_specs=[smem, smem, vmem],
        out_specs=(vmem, smem),
        scratch_shapes=[
            pltpu.VMEM((request_count, message_rows, HDIM), F32),
            pltpu.VMEM((4, request_count, message_rows, HDIM), F32),
            pltpu.VMEM(message, F32),
            pltpu.SMEM((shard_count,), jnp.int32),
        ],
        compiler_params=pltpu.CompilerParams(vmem_limit_bytes=32 * 1024 * 1024),
        name="pack_queries",
    )(neighbour_shard, neighbour_slot, cross_query)
    fresh = step_kv.transpose(1, 0, 2, 3).reshape(2, row_count, width)
    gather_shape = (layer, tensor_count, 2 * share, width // 2)
    out_shape = (share, shard_count, out_weight.shape[1])
    exchange = (x_count, share, layer, out_weight.shape[1])
    dma = pltpu.SemaphoreType.DMA
    self_heads, cross_out = pl.pallas_call(
        main_kernel,
        out_shape=(
            jax.ShapeDtypeStruct((row_count, width), BF16),
            jax.ShapeDtypeStruct(out_shape, BF16),
        ),
        in_specs=[smem] * 4 + [vmem] * 3 + [pl.BlockSpec(memory_space=pl.ANY)] * 2 + [vmem],
        out_specs=(vmem, vmem),
        scratch_shapes=[
            pltpu.VMEM(cache.shape, BF16),
            pltpu.VMEM(corpus_kv.shape, BF16),
            pltpu.VMEM(message, BF16),
            pltpu.VMEM(message, BF16),
            pltpu.VMEM(message, BF16),
            pltpu.VMEM(message, F32),
            pltpu.VMEM(message, F32),
            pltpu.VMEM(gather_shape[1:], BF16),
            pltpu.VMEM(gather_shape, BF16),
            pltpu.VMEM((tensor_count, width, x_count * HDIM), BF16),
            pltpu.VMEM((x_count * layer * share, HDIM), F32),
            pltpu.VMEM(exchange, BF16),
            pltpu.VMEM(exchange, BF16),
            dma((3,)),
            dma, dma((x_count,)),
            dma, dma((x_count,)),
            dma, dma,
            dma((2, max(1, tensor_count // 2))), dma((2, max(1, tensor_count // 2))),
            dma, dma,
            dma, dma((y_count,)),
            dma, dma,
            dma, dma,
        ],
        compiler_params=pltpu.CompilerParams(
            collective_id=0, has_side_effects=True, vmem_limit_bytes=56 * 1024 * 1024
        ),
        name="retrieve_and_project",
    )(
        neighbour_shard, ranks, positions, kv_length,
        send, self_query.reshape(row_count, width), fresh, cache, corpus_kv, out_weight,
    )
    return self_heads.reshape(request_count, step_count, width), cross_out


def solution(mesh):
    return jax.shard_map(
        on_device,
        mesh=mesh,
        in_specs=(
            P("corpus", None, "tensor"),
            P("corpus", None, "tensor"),
            P("corpus", None, None, "tensor"),
            P("corpus", None, None, "tensor"),
            P("corpus"),
            P("corpus"),
            P("corpus", None, None, "tensor"),
            P("corpus", None),
            P("corpus", None),
            P("tensor", "corpus"),
        ),
        out_specs=(P("corpus", None, "tensor"), P("tensor", None, "corpus")),
        check_vma=False,
    )
```

```python
import functools

import jax
import jax.numpy as jnp
from jax import lax
from jax.experimental import pallas as pl
from jax.experimental.pallas import tpu as pltpu
from jax.sharding import PartitionSpec as P

HDIM = 128
NBR = 2
SPAN = 64
CORES = 2
GRID_OF = {64: (4, 8), 8: (2, 2)}
MESH = pl.DeviceIdType.MESH
masked_value = -1e30
F32 = jnp.float32
BF16 = jnp.bfloat16


def pack_queries(shards, slots, query, steps, columns, ranks, total, send_ref):
    item_count, request_count = shards.shape
    shard_count, message_rows, _ = send_ref.shape
    head_count = message_rows // 8
    count = item_count * request_count
    lane = lax.broadcasted_iota(jnp.int32, (1, HDIM), 1)
    shard_row = jnp.full((1, HDIM), -1, jnp.int32)
    tag_row = jnp.zeros((1, HDIM), jnp.int32)
    for number in range(count):
        item, request = divmod(number, request_count)
        shard = shards[item, request]
        shard_row = jnp.where(lane == number, shard, shard_row)
        tag_row = jnp.where(lane == number, slots[item, request] + 1, tag_row)
        columns[number : number + 1, :] = jnp.full((1, HDIM), shard, jnp.int32)
    same = columns[...] == shard_row
    here = lax.broadcasted_iota(jnp.int32, same.shape, 0)
    there = lax.broadcasted_iota(jnp.int32, same.shape, 1)
    ranks[...] = jnp.broadcast_to(
        jnp.sum(jnp.where(same & (there < here), 1.0, 0.0), axis=1, keepdims=True), same.shape
    )
    rank_row = jnp.sum(jnp.where(same & (here < there), 1.0, 0.0), axis=0, keepdims=True)
    for request in range(request_count):
        rows = query[request].astype(F32)
        for step in range(rows.shape[0]):
            steps[step, request : request + 1, :] = rows[step : step + 1, :]
    at_shard = shard_row == lax.broadcasted_iota(jnp.int32, (shard_count, HDIM), 0)
    for rank in range(2):
        chosen = jnp.where(at_shard & (rank_row == rank), 1.0, 0.0)
        tag = jnp.sum(chosen * tag_row.astype(F32), axis=1, keepdims=True)
        tag = jnp.broadcast_to(tag, (shard_count, HDIM))
        for head in range(head_count):
            total[pl.ds(head * 8 + 6 + rank, shard_count, stride=message_rows), :] = tag
        picker = chosen[:, :count].astype(BF16)
        for row in range(3):
            early, late = steps[row], steps[row + 1]
            items = jnp.concatenate([early] * NBR + [late] * NBR, axis=0).astype(BF16)
            packed = jnp.dot(picker, items, preferred_element_type=F32)
            for head in range(head_count):
                start = head * 8 + rank * 3 + row
                total[pl.ds(start, shard_count, stride=message_rows), :] = packed[
                    :, head * HDIM : (head + 1) * HDIM
                ]
    send_ref[...] = total[...].reshape(send_ref.shape).astype(BF16)


def attend_self(query_ref, fresh_ref, cached, length_ref, out_ref, heads):
    request_count, _, cache_length, _ = cached.shape
    row_count, width = query_ref.shape
    step_count = row_count // request_count
    key_count = request_count * cache_length
    row_request = lax.broadcasted_iota(jnp.int32, (row_count, key_count), 0) // step_count
    key_index = lax.broadcasted_iota(jnp.int32, (1, key_count), 1)
    limit = jnp.zeros((1, key_count), jnp.int32)
    for request in range(request_count):
        limit = jnp.where(key_index // cache_length == request, length_ref[request], limit)
    key_request = jnp.where(key_index % cache_length < limit, key_index // cache_length, -1)
    live = row_request == key_request
    fresh_row = lax.broadcasted_iota(jnp.int32, (row_count, row_count), 0)
    fresh_key = lax.broadcasted_iota(jnp.int32, (row_count, row_count), 1)
    fresh_live = (fresh_row // step_count == fresh_key // step_count) & (fresh_key <= fresh_row)
    scale = HDIM ** (-0.5)
    last = (((1,), (1,)), ((), ()))
    for head in heads:
        lanes = slice(head * HDIM, (head + 1) * HDIM)
        query = query_ref[:, lanes].astype(BF16)
        keys = cached[:, 0, :, lanes].reshape(key_count, HDIM)
        values = cached[:, 1, :, lanes].reshape(key_count, HDIM)
        scores = lax.dot_general(query, keys, last, preferred_element_type=F32) * scale
        scores = jnp.where(live, scores, masked_value)
        fresh = lax.dot_general(query, fresh_ref[0, :, lanes].astype(BF16), last, preferred_element_type=F32) * scale
        fresh = jnp.where(fresh_live, fresh, masked_value)
        top = jnp.maximum(
            jnp.max(scores, axis=1, keepdims=True), jnp.max(fresh, axis=1, keepdims=True)
        )
        weights = jnp.exp(scores - top)
        fresh_weights = jnp.exp(fresh - top)
        denom = jnp.sum(weights, axis=1, keepdims=True) + jnp.sum(fresh_weights, axis=1, keepdims=True)
        summed = jnp.dot(weights.astype(BF16), values, preferred_element_type=F32)
        summed = summed + jnp.dot(
            fresh_weights.astype(BF16), fresh_ref[1, :, lanes].astype(BF16), preferred_element_type=F32
        )
        result = summed / denom
        for request in range(request_count):
            rows = result[request * step_count : (request + 1) * step_count, :]
            out_ref[request, :, lanes] = rows.astype(BF16)


def attend_blocks(messages, blocks):
    source_count, message_rows, _ = messages.shape
    head_count = message_rows // 8
    block_count, _, token_count, _ = blocks.shape
    rows = source_count * 8
    scale = HDIM ** (-0.5)
    values = messages.astype(F32)
    in_tile = lax.broadcasted_iota(jnp.int32, (source_count, 8, HDIM), 1)
    lane = lax.broadcasted_iota(jnp.int32, (source_count, 8, HDIM), 2)
    tags = jnp.where(in_tile < 3, values[:, 6:7, :], values[:, 7:8, :]).reshape(rows, HDIM)
    mine = [tags == F32(index + 1) for index in range(block_count)]
    parts = []
    for head in range(head_count):
        lanes = slice(head * HDIM, (head + 1) * HDIM)
        query = values[:, head * 8 : head * 8 + 8, :].reshape(rows, HDIM).astype(BF16)
        keys = blocks[:, 0, :, lanes].reshape(block_count * token_count, HDIM)
        scores = lax.dot_general(
            query, keys, (((1,), (1,)), ((), ())), preferred_element_type=F32
        )
        chosen = jnp.zeros((rows, token_count), F32)
        for index in range(block_count):
            chosen = jnp.where(
                mine[index], scores[:, index * token_count : (index + 1) * token_count], chosen
            )
        chosen = chosen * scale
        top = jnp.max(chosen, axis=1, keepdims=True)
        weights = jnp.exp(chosen - top)
        denom = jnp.sum(weights, axis=1, keepdims=True)
        spread = jnp.concatenate(
            [jnp.where(mine[index], weights, 0.0).astype(BF16) for index in range(block_count)], axis=1
        )
        held = blocks[:, 1, :, lanes].reshape(block_count * token_count, HDIM)
        summed = jnp.dot(spread, held, preferred_element_type=F32) / denom
        level = jnp.broadcast_to(top + jnp.log(denom), (rows, HDIM)).reshape(source_count, 8, HDIM)
        level = jnp.sum(jnp.where(lane % 8 == in_tile, level, 0.0), axis=1, keepdims=True)
        high = level.astype(BF16).astype(F32)
        middle = (level - high).astype(BF16).astype(F32)
        low = level - high - middle
        terms = jnp.where(lane < 8, high, jnp.where(lane < 16, middle, low))
        parts.append(jnp.where(in_tile == 6, terms, summed.reshape(source_count, 8, HDIM)))
    return jnp.concatenate(parts, axis=1).astype(BF16)


def row_levels(values):
    source_count, message_rows, _ = values.shape
    tiles = values.reshape(source_count * message_rows // 8, 8, HDIM)
    in_tile = lax.broadcasted_iota(jnp.int32, tiles.shape, 1)
    lane = lax.broadcasted_iota(jnp.int32, tiles.shape, 2)
    terms = jnp.broadcast_to(tiles[:, 6:7, :], tiles.shape)
    picked = jnp.where((lane < 24) & (lane % 8 == in_tile), terms, 0.0)
    levels = jnp.sum(picked, axis=2, keepdims=True)
    return jnp.broadcast_to(levels, tiles.shape).reshape(values.shape)


def main_kernel(
    shard_ref, slot_ref, position_ref, length_ref,
    cross_ref, query_ref, fresh_ref, cache_ref, corpus_ref, weight_ref,
    self_ref, out_ref,
    shards, slots, cross, query, fresh, query_rows, fresh_rows, steps, columns, ranks, packed,
    cached, blocks, send, arrived, reply, returned, sums, levels,
    heads, gathered, weights, totals, out_send, out_recv,
    entered, local_sem, query_send, query_recv, reply_send, reply_recv,
    x_send, x_recv, ring_send, ring_recv, head_send, head_recv,
    y_send, y_recv, core_send, core_recv, out_send_sem, out_recv_sem,
):
    shard_count, message_rows, _ = send.shape
    x_count, y_count = GRID_OF[shard_count]
    layer = y_count * CORES
    tensor_count = gathered.shape[1]
    request_count, step_count, _ = cross.shape
    me, mine = lax.axis_index("corpus"), lax.axis_index("tensor")
    x = me // layer
    y = (me // CORES) % y_count
    core = me % CORES

    def device_at(dx, dy, dc):
        return (((x + dx) % x_count) * y_count + (y + dy) % y_count) * CORES + (core + dc) % CORES

    def remote(source, target, send_sem, recv_sem, corpus=None, tensor=None):
        return pltpu.make_async_remote_copy(
            src_ref=source,
            dst_ref=target,
            send_sem=send_sem,
            recv_sem=recv_sem,
            device_id=(me if corpus is None else corpus, mine if tensor is None else tensor),
            device_id_type=MESH,
        )

    def wait_bytes(ref, sem):
        pltpu.make_async_copy(ref, ref, sem).wait()

    small = [
        pltpu.make_async_copy(source, target, local_sem.at[index])
        for index, (source, target) in enumerate(
            [(shard_ref, shards), (slot_ref, slots), (cross_ref, cross), (query_ref, query),
             (fresh_ref, fresh)]
        )
    ]
    for copy in small:
        copy.start()

    barrier = pltpu.get_barrier_semaphore()

    def greet(sem, corpus, tensor):
        pl.semaphore_signal(sem, inc=1, device_id=(corpus, tensor), device_id_type=MESH)

    for dx in range(1, x_count):
        greet(barrier, device_at(dx, 0, 0), mine)

    def greet_layer(step, carry):
        greet(barrier, device_at(0, step // CORES, step % CORES), mine)
        return carry

    def greet_tensor(step, carry):
        greet(barrier, me, (mine + step) % tensor_count)
        return carry

    lax.fori_loop(1, layer, greet_layer, 0)
    lax.fori_loop(1, tensor_count, greet_tensor, 0)
    own_weight = pltpu.make_async_copy(weight_ref, weights.at[mine, x], local_sem.at[5])
    own_weight.start()
    cache_copy = pltpu.make_async_copy(cache_ref, cached, local_sem.at[6])
    corpus_copy = pltpu.make_async_copy(corpus_ref, blocks, local_sem.at[7])
    cache_copy.start()
    corpus_copy.start()
    for copy in small:
        copy.wait()
    pack_queries(shards, slots, cross, steps, columns, ranks, packed, send)
    own_query = pltpu.make_async_copy(send.at[me], arrived.at[me], query_recv.at[0])
    own_query.start()
    pl.semaphore_wait(barrier, x_count - 1 + layer - 1 + tensor_count - 1)
    for dx in range(1, x_count):
        greet(entered, device_at(dx, 0, 0), mine)
    own_weight.wait()

    for dx in range(1, x_count):
        remote(
            weight_ref, weights.at[mine, x], x_send, x_recv.at[dx], device_at(dx, 0, 0)
        ).start()
    ups, downs = tensor_count // 2, (tensor_count - 1) // 2

    def ring_copy(down, step, offset):
        owner = (mine + (step if down else tensor_count - step)) % tensor_count
        piece = weights.at[owner, (x + offset) % x_count]
        after = (mine + (tensor_count - 1 if down else 1)) % tensor_count
        return remote(
            piece, piece, ring_send.at[down, step, offset], ring_recv.at[down, step, offset],
            tensor=after,
        )

    def ring_wait(step, offset):
        if 0 <= step < ups:
            ring_copy(0, step, offset).wait_recv()
        if 0 <= step < downs:
            ring_copy(1, step, offset).wait_recv()

    def ring_step(step, offset):
        ring_wait(step - 1, offset)
        if step < ups:
            ring_copy(0, step, offset).start()
        if step < downs:
            ring_copy(1, step, offset).start()

    ring_step(0, 0)
    pl.semaphore_wait(entered, x_count - 1)

    def send_queries(dx, first):
        def body(step, carry):
            target = device_at(dx, step // CORES, step % CORES)
            remote(
                send.at[target], arrived.at[me], query_send, query_recv.at[dx], target
            ).start()
            return carry

        lax.fori_loop(first, layer, body, 0)

    for dx in range(x_count):
        send_queries(dx, 1 if dx == 0 else 0)

    for request in range(request_count):
        rows = slice(request * step_count, (request + 1) * step_count)
        query_rows[rows, :] = query[request].astype(F32)
        for index in range(2):
            fresh_rows[index, rows, :] = fresh[request, index].astype(F32)
    cache_copy.wait()
    all_heads = range(message_rows // 8)
    attend_self(query_rows, fresh_rows, cached, length_ref, self_ref, all_heads[:2])
    for offset in range(1, x_count):
        wait_bytes(weights.at[mine, (x + offset) % x_count], x_recv.at[x_count - offset])
        ring_step(0, offset)
    attend_self(query_rows, fresh_rows, cached, length_ref, self_ref, all_heads[2:])
    corpus_copy.wait()

    def serve(dx, carry):
        first = pl.multiple_of(((x - dx + x_count) % x_count) * layer, layer)
        chunk = pl.ds(first, layer)
        wait_bytes(arrived.at[chunk], query_recv.at[dx])
        reply[chunk] = attend_blocks(arrived[chunk], blocks)

        def answer(step, inner):
            target = device_at(x_count - dx, step // CORES, step % CORES)
            remote(
                reply.at[target], returned.at[me], reply_send, reply_recv.at[dx], target
            ).start()
            return inner

        lax.fori_loop(jnp.where(dx == 0, 1, 0), layer, answer, 0)
        ring_step(1, dx)
        return carry

    lax.fori_loop(0, x_count, serve, 0)
    own_reply = pltpu.make_async_copy(reply.at[me], returned.at[me], reply_recv.at[0])
    own_reply.start()

    def decode(dx, carry):
        first = pl.multiple_of(((x + dx) % x_count) * layer, layer)
        chunk = pl.ds(first, layer)
        wait_bytes(returned.at[chunk], reply_recv.at[dx])
        values = returned[chunk].astype(F32)
        sums[chunk] = values
        levels[chunk] = row_levels(values)
        ring_step(2, dx)
        return carry

    lax.fori_loop(0, x_count, decode, 0)

    tile_row = lax.broadcasted_iota(jnp.int32, (message_rows, HDIM), 0) % 8

    def combined(request):
        boundary = SPAN - position_ref[request] % SPAN
        late = tile_row >= boundary

        def item(ref, number):
            tile = ref[shards[number, request]]
            second = ranks[pl.ds(number * request_count + request, 1), :] == 1.0
            if number < NBR:
                return jnp.where(second, pltpu.roll(tile, message_rows - 3, 0), tile)
            return jnp.where(
                second, pltpu.roll(tile, message_rows - 2, 0), pltpu.roll(tile, 1, 0)
            )

        def pair(ref):
            return [
                jnp.where(late, item(ref, NBR + number), item(ref, number)) for number in range(NBR)
            ]

        held, level = pair(sums), pair(levels)
        joint = jnp.maximum(level[0], level[1])
        factors = [jnp.exp(entry - joint) for entry in level]
        return (factors[0] * held[0] + factors[1] * held[1]) / (factors[0] + factors[1])

    def combine(owner, carry):
        first = combined(owner * 2)
        second = pltpu.roll(combined(owner * 2 + 1), 4, 0)
        both = jnp.where(tile_row < 4, first, second)
        upper = jnp.concatenate([both[0:8], both[8:16]], axis=1)
        lower = jnp.concatenate([both[16:24], both[24:32]], axis=1)
        heads[owner] = jnp.concatenate([upper, lower], axis=0).astype(BF16)
        return carry

    lax.fori_loop(0, tensor_count, combine, 0)

    place = y * CORES + core
    own_heads = pltpu.make_async_copy(heads.at[mine], gathered.at[place, mine], head_recv)
    own_heads.start()

    def send_heads(step, carry):
        owner = (mine + step) % tensor_count
        remote(
            heads.at[owner], gathered.at[place, mine], head_send, head_recv, tensor=owner
        ).start()
        return carry

    lax.fori_loop(1, tensor_count, send_heads, 0)
    ring_step(3, 0)
    wait_bytes(gathered.at[place], head_recv)

    def slot_at(dy):
        return ((y + dy) % y_count) * CORES + core

    def send_y(ref, dy, number):
        return remote(ref, ref, y_send.at[number], y_recv.at[number], device_at(0, dy, 0))

    def pass_core(index):
        remote(
            gathered.at[index], gathered.at[index], core_send, core_recv, device_at(0, 0, 1)
        ).start()

    own = gathered.at[place]
    if y_count == 8:
        halves = (pl.ds(0, tensor_count // 2), pl.ds(tensor_count // 2, tensor_count // 2))
        far_low, far_high = (gathered.at[slot_at(4), half] for half in halves)
        first = [send_y(own, 2, 1), send_y(own, -2 + y_count, 3), send_y(own, 1, 0),
                 send_y(own, y_count - 1, 2)]
        for copy in first:
            copy.start()
        pass_core(place)
        ring_step(3, 1)
        below, above = gathered.at[slot_at(y_count - 2)], gathered.at[slot_at(2)]
        wait_bytes(below, y_recv.at[1])
        second = [send_y(gathered.at[slot_at(y_count - 2), halves[0]], 2, 6), send_y(below, 1, 4)]
        for copy in second:
            copy.start()
        wait_bytes(above, y_recv.at[3])
        third = [send_y(gathered.at[slot_at(2), halves[1]], y_count - 2, 7),
                 send_y(above, y_count - 1, 5)]
        for copy in third:
            copy.start()
        pass_core(slot_at(y_count - 2))
        pass_core(slot_at(2))
        for dy, number in ((y_count - 1, 0), (1, 2)):
            wait_bytes(gathered.at[slot_at(dy)], y_recv.at[number])
            pass_core(slot_at(dy))
        ring_step(3, 2)
        ring_step(3, 3)
        for dy, number in ((y_count - 3, 4), (3, 5)):
            wait_bytes(gathered.at[slot_at(dy)], y_recv.at[number])
            pass_core(slot_at(dy))
        wait_bytes(far_low, y_recv.at[6])
        wait_bytes(far_high, y_recv.at[7])
        pass_core(slot_at(4))
        y_copies = first + second + third
    else:
        y_copies = [send_y(own, dy, dy) for dy in range(1, y_count)]
        for copy in y_copies:
            copy.start()
        pass_core(place)
        for dy in range(1, y_count):
            wait_bytes(gathered.at[slot_at(y_count - dy)], y_recv.at[dy])
            pass_core(slot_at(y_count - dy))
        for offset in range(1, x_count):
            ring_step(3, offset)
    for offset in range(x_count):
        ring_wait(3, offset)
    wait_bytes(gathered.at[pl.ds(0, y_count)], core_recv)

    half = gathered.shape[2] // 2
    rows = layer * half

    def project(owner):
        block = gathered[:, owner].astype(F32)
        left = jnp.concatenate(
            [block[:, :half].reshape(rows, -1), block[:, half:].reshape(rows, -1)], axis=1
        ).astype(BF16)
        right = jnp.concatenate([weights[owner, index] for index in range(x_count)], axis=1)
        return jnp.dot(left, right, preferred_element_type=F32)

    totals[...] = jnp.zeros_like(totals)

    def accumulate(owner, carry):
        product = project(owner)
        for dx in range(x_count):
            totals[dx * rows : (dx + 1) * rows, :] += product[:, dx * HDIM : (dx + 1) * HDIM]
        return carry

    lax.fori_loop(0, tensor_count, accumulate, 0)
    for row in range(half):
        for index in range(x_count):
            picked = totals[pl.ds(index * rows + row, layer, stride=half), :]
            out_send[index, row] = picked.astype(BF16)
    own_out = pltpu.make_async_copy(out_send.at[x], out_recv.at[x], out_recv_sem)
    own_out.start()
    for dx in range(1, x_count):
        remote(
            out_send.at[(x + dx) % x_count], out_recv.at[x], out_send_sem, out_recv_sem,
            device_at(dx, 0, 0),
        ).start()
    wait_bytes(out_recv, out_recv_sem)
    for index in range(x_count):
        out_ref[:, index * layer : (index + 1) * layer, :] = out_recv[index]

    wait_bytes(send.at[pl.ds(0, shard_count - 1)], query_send)
    wait_bytes(reply.at[pl.ds(0, shard_count - 1)], reply_send)
    wait_bytes(weights.at[mine, pl.ds(0, x_count - 1)], x_send)
    for down, length in ((0, ups), (1, downs)):
        for step in range(length):
            for offset in range(x_count):
                ring_copy(down, step, offset).wait_send()
    wait_bytes(heads.at[pl.ds(0, tensor_count - 1)], head_send)
    for copy in y_copies:
        copy.wait_send()
    wait_bytes(gathered.at[pl.ds(0, y_count)], core_send)
    wait_bytes(out_send.at[pl.ds(0, x_count - 1)], out_send_sem)


def on_device(
    self_query,
    cross_query,
    cache,
    step_kv,
    kv_length,
    positions,
    corpus_kv,
    neighbour_shard,
    neighbour_slot,
    out_weight,
):
    request_count, step_count, width = cross_query.shape
    head_count = width // HDIM
    shard_count = lax.axis_size("corpus")
    tensor_count = lax.axis_size("tensor")
    x_count, y_count = GRID_OF[shard_count]
    layer = y_count * CORES
    message_rows = head_count * 8
    row_count = request_count * step_count
    share = row_count // tensor_count
    smem = pl.BlockSpec(memory_space=pltpu.SMEM)
    vmem = pl.BlockSpec(memory_space=pltpu.VMEM)
    hbm = pl.BlockSpec(memory_space=pl.ANY)
    message = (shard_count, message_rows, HDIM)
    gather_shape = (layer, tensor_count, 2 * share, width // 2)
    out_shape = (share, shard_count, out_weight.shape[1])
    exchange = (x_count, share, layer, out_weight.shape[1])
    dma = pltpu.SemaphoreType.DMA
    ring_shape = (2, max(1, tensor_count // 2), x_count)
    self_heads, cross_out = pl.pallas_call(
        main_kernel,
        out_shape=(
            jax.ShapeDtypeStruct(self_query.shape, BF16),
            jax.ShapeDtypeStruct(out_shape, BF16),
        ),
        in_specs=[hbm] * 2 + [smem] * 2 + [hbm] * 6,
        out_specs=(vmem, vmem),
        scratch_shapes=[
            pltpu.SMEM((2 * NBR, request_count), jnp.int32),
            pltpu.SMEM((2 * NBR, request_count), jnp.int32),
            pltpu.VMEM(cross_query.shape, BF16),
            pltpu.VMEM(self_query.shape, BF16),
            pltpu.VMEM(step_kv.shape, BF16),
            pltpu.VMEM((row_count, width), F32),
            pltpu.VMEM((2, row_count, width), F32),
            pltpu.VMEM((step_count, request_count, width), F32),
            pltpu.VMEM((2 * NBR * request_count, HDIM), jnp.int32),
            pltpu.VMEM((2 * NBR * request_count, HDIM), F32),
            pltpu.VMEM((shard_count * message_rows, HDIM), F32),
            pltpu.VMEM(cache.shape, BF16),
            pltpu.VMEM(corpus_kv.shape, BF16),
            pltpu.VMEM(message, BF16),
            pltpu.VMEM(message, BF16),
            pltpu.VMEM(message, BF16),
            pltpu.VMEM(message, BF16),
            pltpu.VMEM(message, F32),
            pltpu.VMEM(message, F32),
            pltpu.VMEM(gather_shape[1:], BF16),
            pltpu.VMEM(gather_shape, BF16),
            pltpu.VMEM((tensor_count, x_count, width, HDIM), BF16),
            pltpu.VMEM((x_count * layer * share, HDIM), F32),
            pltpu.VMEM(exchange, BF16),
            pltpu.VMEM(exchange, BF16),
            pltpu.SemaphoreType.REGULAR,
            dma((8,)),
            dma, dma((x_count,)),
            dma, dma((x_count,)),
            dma, dma((x_count,)),
            dma(ring_shape), dma(ring_shape),
            dma, dma,
            dma((8,)), dma((8,)),
            dma, dma,
            dma, dma,
        ],
        compiler_params=pltpu.CompilerParams(
            collective_id=0, has_side_effects=True, vmem_limit_bytes=56 * 1024 * 1024
        ),
        name="retrieve_and_project",
    )(
        neighbour_shard.T, neighbour_slot.T, positions, kv_length,
        cross_query, self_query, step_kv, cache, corpus_kv, out_weight,
    )
    return self_heads, cross_out


def solution(mesh):
    return jax.shard_map(
        on_device,
        mesh=mesh,
        in_specs=(
            P("corpus", None, "tensor"),
            P("corpus", None, "tensor"),
            P("corpus", None, None, "tensor"),
            P("corpus", None, None, "tensor"),
            P("corpus"),
            P("corpus"),
            P("corpus", None, None, "tensor"),
            P("corpus", None),
            P("corpus", None),
            P("tensor", "corpus"),
        ),
        out_specs=(P("corpus", None, "tensor"), P("tensor", None, "corpus")),
        check_vma=False,
    )
```

```python
import functools

import jax
import jax.numpy as jnp
from jax import lax
from jax.experimental import pallas as pl
from jax.experimental.pallas import tpu as pltpu
from jax.sharding import PartitionSpec as P

HDIM = 128
NBR = 2
SPAN = 64
CORES = 2
GRID_OF = {64: (4, 8), 8: (2, 2)}
MESH = pl.DeviceIdType.MESH
masked_value = -1e30
F32 = jnp.float32
BF16 = jnp.bfloat16


def pack_queries(shards, slots, query, steps, columns, ranks, total, send_ref):
    item_count, request_count = shards.shape
    shard_count, message_rows, _ = send_ref.shape
    head_count = message_rows // 8
    count = item_count * request_count
    lane = lax.broadcasted_iota(jnp.int32, (1, HDIM), 1)
    shard_row = jnp.full((1, HDIM), -1, jnp.int32)
    tag_row = jnp.zeros((1, HDIM), jnp.int32)
    for number in range(count):
        item, request = divmod(number, request_count)
        shard = shards[item, request]
        shard_row = jnp.where(lane == number, shard, shard_row)
        tag_row = jnp.where(lane == number, slots[item, request] + 1, tag_row)
        columns[number : number + 1, :] = jnp.full((1, HDIM), shard, jnp.int32)
    same = columns[...] == shard_row
    here = lax.broadcasted_iota(jnp.int32, same.shape, 0)
    there = lax.broadcasted_iota(jnp.int32, same.shape, 1)
    ranks[...] = jnp.broadcast_to(
        jnp.sum(jnp.where(same & (there < here), 1.0, 0.0), axis=1, keepdims=True), same.shape
    )
    rank_row = jnp.sum(jnp.where(same & (here < there), 1.0, 0.0), axis=0, keepdims=True)
    for request in range(request_count):
        rows = query[request].astype(F32)
        for step in range(rows.shape[0]):
            steps[step, request : request + 1, :] = rows[step : step + 1, :]
    at_shard = shard_row == lax.broadcasted_iota(jnp.int32, (shard_count, HDIM), 0)
    for rank in range(2):
        chosen = jnp.where(at_shard & (rank_row == rank), 1.0, 0.0)
        tag = jnp.sum(chosen * tag_row.astype(F32), axis=1, keepdims=True)
        tag = jnp.broadcast_to(tag, (shard_count, HDIM))
        for head in range(head_count):
            total[pl.ds(head * 8 + 6 + rank, shard_count, stride=message_rows), :] = tag
        picker = chosen[:, :count].astype(BF16)
        for row in range(3):
            early, late = steps[row], steps[row + 1]
            items = jnp.concatenate([early] * NBR + [late] * NBR, axis=0).astype(BF16)
            packed = jnp.dot(picker, items, preferred_element_type=F32)
            for head in range(head_count):
                start = head * 8 + rank * 3 + row
                total[pl.ds(start, shard_count, stride=message_rows), :] = packed[
                    :, head * HDIM : (head + 1) * HDIM
                ]
    send_ref[...] = total[...].reshape(send_ref.shape).astype(BF16)


def attend_self(query_ref, fresh_ref, cached, length_ref, out_ref, heads):
    request_count, _, cache_length, _ = cached.shape
    row_count, width = query_ref.shape
    step_count = row_count // request_count
    key_count = request_count * cache_length
    row_request = lax.broadcasted_iota(jnp.int32, (row_count, key_count), 0) // step_count
    key_index = lax.broadcasted_iota(jnp.int32, (1, key_count), 1)
    limit = jnp.zeros((1, key_count), jnp.int32)
    for request in range(request_count):
        limit = jnp.where(key_index // cache_length == request, length_ref[request], limit)
    key_request = jnp.where(key_index % cache_length < limit, key_index // cache_length, -1)
    live = row_request == key_request
    fresh_row = lax.broadcasted_iota(jnp.int32, (row_count, row_count), 0)
    fresh_key = lax.broadcasted_iota(jnp.int32, (row_count, row_count), 1)
    fresh_live = (fresh_row // step_count == fresh_key // step_count) & (fresh_key <= fresh_row)
    scale = HDIM ** (-0.5)
    last = (((1,), (1,)), ((), ()))
    for head in heads:
        lanes = slice(head * HDIM, (head + 1) * HDIM)
        query = query_ref[:, lanes].astype(BF16)
        keys = cached[:, 0, :, lanes].reshape(key_count, HDIM)
        values = cached[:, 1, :, lanes].reshape(key_count, HDIM)
        scores = lax.dot_general(query, keys, last, preferred_element_type=F32) * scale
        scores = jnp.where(live, scores, masked_value)
        fresh = lax.dot_general(query, fresh_ref[0, :, lanes].astype(BF16), last, preferred_element_type=F32) * scale
        fresh = jnp.where(fresh_live, fresh, masked_value)
        top = jnp.maximum(
            jnp.max(scores, axis=1, keepdims=True), jnp.max(fresh, axis=1, keepdims=True)
        )
        weights = jnp.exp(scores - top)
        fresh_weights = jnp.exp(fresh - top)
        denom = jnp.sum(weights, axis=1, keepdims=True) + jnp.sum(fresh_weights, axis=1, keepdims=True)
        summed = jnp.dot(weights.astype(BF16), values, preferred_element_type=F32)
        summed = summed + jnp.dot(
            fresh_weights.astype(BF16), fresh_ref[1, :, lanes].astype(BF16), preferred_element_type=F32
        )
        result = summed / denom
        for request in range(request_count):
            rows = result[request * step_count : (request + 1) * step_count, :]
            out_ref[request, :, lanes] = rows.astype(BF16)


def attend_blocks(messages, blocks):
    source_count, message_rows, _ = messages.shape
    head_count = message_rows // 8
    block_count, _, token_count, _ = blocks.shape
    rows = source_count * 8
    scale = HDIM ** (-0.5)
    values = messages.astype(F32)
    in_tile = lax.broadcasted_iota(jnp.int32, (source_count, 8, HDIM), 1)
    lane = lax.broadcasted_iota(jnp.int32, (source_count, 8, HDIM), 2)
    tags = jnp.where(in_tile < 3, values[:, 6:7, :], values[:, 7:8, :]).reshape(rows, HDIM)
    mine = [tags == F32(index + 1) for index in range(block_count)]
    parts = []
    for head in range(head_count):
        lanes = slice(head * HDIM, (head + 1) * HDIM)
        query = values[:, head * 8 : head * 8 + 8, :].reshape(rows, HDIM).astype(BF16)
        keys = blocks[:, 0, :, lanes].reshape(block_count * token_count, HDIM)
        scores = lax.dot_general(
            query, keys, (((1,), (1,)), ((), ())), preferred_element_type=F32
        )
        chosen = jnp.zeros((rows, token_count), F32)
        for index in range(block_count):
            chosen = jnp.where(
                mine[index], scores[:, index * token_count : (index + 1) * token_count], chosen
            )
        chosen = chosen * scale
        top = jnp.max(chosen, axis=1, keepdims=True)
        weights = jnp.exp(chosen - top)
        denom = jnp.sum(weights, axis=1, keepdims=True)
        spread = jnp.concatenate(
            [jnp.where(mine[index], weights, 0.0).astype(BF16) for index in range(block_count)], axis=1
        )
        held = blocks[:, 1, :, lanes].reshape(block_count * token_count, HDIM)
        summed = jnp.dot(spread, held, preferred_element_type=F32) / denom
        level = jnp.broadcast_to(top + jnp.log(denom), (rows, HDIM)).reshape(source_count, 8, HDIM)
        level = jnp.sum(jnp.where(lane % 8 == in_tile, level, 0.0), axis=1, keepdims=True)
        high = level.astype(BF16).astype(F32)
        middle = (level - high).astype(BF16).astype(F32)
        low = level - high - middle
        terms = jnp.where(lane < 8, high, jnp.where(lane < 16, middle, low))
        parts.append(jnp.where(in_tile == 6, terms, summed.reshape(source_count, 8, HDIM)))
    return jnp.concatenate(parts, axis=1).astype(BF16)


def row_levels(values):
    source_count, message_rows, _ = values.shape
    tiles = values.reshape(source_count * message_rows // 8, 8, HDIM)
    in_tile = lax.broadcasted_iota(jnp.int32, tiles.shape, 1)
    lane = lax.broadcasted_iota(jnp.int32, tiles.shape, 2)
    terms = jnp.broadcast_to(tiles[:, 6:7, :], tiles.shape)
    picked = jnp.where((lane < 24) & (lane % 8 == in_tile), terms, 0.0)
    levels = jnp.sum(picked, axis=2, keepdims=True)
    return jnp.broadcast_to(levels, tiles.shape).reshape(values.shape)


def main_kernel(
    shard_ref, slot_ref, position_ref, length_ref,
    cross_ref, query_ref, fresh_ref, cache_ref, corpus_ref, weight_ref,
    self_ref, out_ref,
    shards, slots, cross, query, fresh, query_rows, fresh_rows, steps, columns, ranks, packed,
    cached, blocks, send, arrived, reply, returned, sums, levels,
    heads, gathered, weights, totals, out_send, out_recv,
    entered, local_sem, query_send, query_recv, reply_send, reply_recv,
    x_send, x_recv, ring_send, ring_recv, head_send, head_recv,
    y_send, y_recv, core_send, core_recv, out_send_sem, out_recv_sem,
):
    shard_count, message_rows, _ = send.shape
    x_count, y_count = GRID_OF[shard_count]
    layer = y_count * CORES
    tensor_count = heads.shape[0]
    request_count, step_count, _ = cross.shape
    me, mine = lax.axis_index("corpus"), lax.axis_index("tensor")
    x = me // layer
    y = (me // CORES) % y_count
    core = me % CORES
    turn = (x + mine) % 2

    def device_at(dx, dy, dc):
        return (((x + dx) % x_count) * y_count + (y + dy) % y_count) * CORES + (core + dc) % CORES

    def remote(source, target, send_sem, recv_sem, corpus=None, tensor=None):
        return pltpu.make_async_remote_copy(
            src_ref=source,
            dst_ref=target,
            send_sem=send_sem,
            recv_sem=recv_sem,
            device_id=(me if corpus is None else corpus, mine if tensor is None else tensor),
            device_id_type=MESH,
        )

    def wait_bytes(ref, sem):
        pltpu.make_async_copy(ref, ref, sem).wait()

    small = [
        pltpu.make_async_copy(source, target, local_sem.at[index])
        for index, (source, target) in enumerate(
            [(shard_ref, shards), (slot_ref, slots), (cross_ref, cross), (query_ref, query),
             (fresh_ref, fresh)]
        )
    ]
    for copy in small:
        copy.start()

    barrier = pltpu.get_barrier_semaphore()

    def greet(sem, corpus, tensor):
        pl.semaphore_signal(sem, inc=1, device_id=(corpus, tensor), device_id_type=MESH)

    for dx in range(1, x_count):
        greet(barrier, device_at(dx, 0, 0), mine)

    def greet_layer(step, carry):
        greet(barrier, device_at(0, step // CORES, step % CORES), mine)
        return carry

    def greet_tensor(step, carry):
        greet(barrier, me, (mine + step) % tensor_count)
        return carry

    lax.fori_loop(1, layer, greet_layer, 0)
    lax.fori_loop(1, tensor_count, greet_tensor, 0)
    own_place = weights.at[mine // 2, x]
    own_weight = pltpu.make_async_copy(weight_ref, own_place, local_sem.at[5])
    pl.when(turn == 0)(own_weight.start)
    cache_copy = pltpu.make_async_copy(cache_ref, cached, local_sem.at[6])
    corpus_copy = pltpu.make_async_copy(corpus_ref, blocks, local_sem.at[7])
    cache_copy.start()
    corpus_copy.start()
    pl.semaphore_wait(barrier, x_count - 1 + layer - 1 + tensor_count - 1)
    for dx in range(1, x_count):
        greet(entered, device_at(dx, 0, 0), mine)

    def send_weight(dx):
        remote(
            weight_ref, weights.at[mine // 2, x], x_send, x_recv.at[dx], device_at(dx, 0, 0)
        ).start()

    odd_steps, even_steps = range(1, x_count, 2), range(2, x_count, 2)

    @pl.when(turn == 1)
    def _():
        for dx in odd_steps:
            send_weight(dx)

    @pl.when(turn == 0)
    def _():
        for dx in even_steps:
            send_weight(dx)

    last_step, half_count = tensor_count // 2 - 1, x_count // 2

    def ring_copy(down, step, offset):
        owner = (mine + (step if down else tensor_count - step)) % tensor_count
        piece = weights.at[owner // 2, (x + offset) % x_count]
        after = (mine + (tensor_count - 1 if down else 1)) % tensor_count
        return remote(
            piece, piece, ring_send.at[down, step, offset], ring_recv.at[down, step, offset],
            tensor=after,
        )

    def ring_ways(step, offset):
        if step == last_step:
            return (0,) if offset < half_count else (1,)
        return (0, 1) if 0 <= step < last_step else ()

    def ring_wait(step, offset):
        for down in ring_ways(step, offset):
            ring_copy(down, step, offset).wait_recv()

    def ring_step(step, offset):
        if step > last_step:
            return

        @pl.when((turn + step) % 2 == 0)
        def _():
            ring_wait(step - 1, offset)
            for down in ring_ways(step, offset):
                ring_copy(down, step, offset).start()

    pl.when(turn == 0)(own_weight.wait)
    ring_step(0, 0)
    for copy in small:
        copy.wait()
    pack_queries(shards, slots, cross, steps, columns, ranks, packed, send)
    own_query = pltpu.make_async_copy(send.at[me], arrived.at[me], query_recv.at[0])
    own_query.start()
    ring_step(1, 0)
    pl.semaphore_wait(entered, x_count - 1)

    def send_queries(dx, first):
        def body(step, carry):
            target = device_at(dx, step // CORES, step % CORES)
            remote(
                send.at[target], arrived.at[me], query_send, query_recv.at[dx], target
            ).start()
            return carry

        lax.fori_loop(first, layer, body, 0)

    for dx in range(x_count):
        send_queries(dx, 1 if dx == 0 else 0)

    for request in range(request_count):
        rows = slice(request * step_count, (request + 1) * step_count)
        query_rows[rows, :] = query[request].astype(F32)
        for index in range(2):
            fresh_rows[index, rows, :] = fresh[request, index].astype(F32)
    cache_copy.wait()
    all_heads = range(message_rows // 8)

    for offset in range(1, x_count):
        @pl.when(turn == 0)
        def _():
            source = weights.at[mine // 2, (x + offset) % x_count]
            wait_bytes(source, x_recv.at[x_count - offset])

        ring_step(0, offset)
    attend_self(query_rows, fresh_rows, cached, length_ref, self_ref, all_heads[:2])
    ring_step(2, 0)
    attend_self(query_rows, fresh_rows, cached, length_ref, self_ref, all_heads[2:])
    ring_step(1, 1)
    corpus_copy.wait()

    def serve(dx, carry):
        first = pl.multiple_of(((x - dx + x_count) % x_count) * layer, layer)
        chunk = pl.ds(first, layer)
        wait_bytes(arrived.at[chunk], query_recv.at[dx])
        reply[chunk] = attend_blocks(arrived[chunk], blocks)

        def answer(step, inner):
            target = device_at(x_count - dx, step // CORES, step % CORES)
            remote(
                reply.at[target], returned.at[me], reply_send, reply_recv.at[dx], target
            ).start()
            return inner

        lax.fori_loop(jnp.where(dx == 0, 1, 0), layer, answer, 0)
        if last_step > 0:
            for index, (step, offset) in enumerate(((1, 2), (1, 3), (2, 1), (2, 2))):
                pl.when(dx == index)(functools.partial(ring_step, step, offset))
        return carry

    lax.fori_loop(0, x_count, serve, 0)
    own_reply = pltpu.make_async_copy(reply.at[me], returned.at[me], reply_recv.at[0])
    own_reply.start()
    ring_step(3, 0)

    def decode(dx, carry):
        first = pl.multiple_of(((x + dx) % x_count) * layer, layer)
        chunk = pl.ds(first, layer)
        wait_bytes(returned.at[chunk], reply_recv.at[dx])
        values = returned[chunk].astype(F32)
        sums[chunk] = values
        levels[chunk] = row_levels(values)
        if last_step > 1:
            for index, (step, offset) in ((0, (2, 3)), (1, (3, 1)), (2, (3, 2)), (3, (3, 3))):
                pl.when(dx == index)(functools.partial(ring_step, step, offset))
        return carry

    lax.fori_loop(0, x_count, decode, 0)

    tile_row = lax.broadcasted_iota(jnp.int32, (message_rows, HDIM), 0) % 8

    def combined(request):
        boundary = SPAN - position_ref[request] % SPAN
        late = tile_row >= boundary

        def item(ref, number):
            tile = ref[shards[number, request]]
            second = ranks[pl.ds(number * request_count + request, 1), :] == 1.0
            if number < NBR:
                return jnp.where(second, pltpu.roll(tile, message_rows - 3, 0), tile)
            return jnp.where(
                second, pltpu.roll(tile, message_rows - 2, 0), pltpu.roll(tile, 1, 0)
            )

        def pair(ref):
            return [
                jnp.where(late, item(ref, NBR + number), item(ref, number)) for number in range(NBR)
            ]

        held, level = pair(sums), pair(levels)
        joint = jnp.maximum(level[0], level[1])
        factors = [jnp.exp(entry - joint) for entry in level]
        return (factors[0] * held[0] + factors[1] * held[1]) / (factors[0] + factors[1])

    def combine(owner, carry):
        first = combined(owner * 2)
        second = pltpu.roll(combined(owner * 2 + 1), 4, 0)
        both = jnp.where(tile_row < 4, first, second)
        upper = jnp.concatenate([both[0:8], both[8:16]], axis=1)
        lower = jnp.concatenate([both[16:24], both[24:32]], axis=1)
        heads[owner] = jnp.concatenate([upper, lower], axis=0).astype(BF16)
        return carry

    lax.fori_loop(0, tensor_count, combine, 0)

    place = y * CORES + core
    taker = device_at(jnp.where(x % 2 == 0, turn, x_count - turn), 0, 0)

    def head_copy(owner):
        return remote(
            heads.at[owner], gathered.at[place, x % 2, mine // 2], head_send, head_recv,
            taker, owner,
        )

    own_heads = pltpu.make_async_copy(
        heads.at[mine], gathered.at[place, x % 2, mine // 2], head_recv
    )
    pl.when(turn == 0)(own_heads.start)

    @pl.when(turn == 1)
    def _():
        head_copy(mine).start()

    def send_heads(step, carry):
        head_copy((mine + step) % tensor_count).start()
        return carry

    lax.fori_loop(1, tensor_count, send_heads, 0)
    wait_bytes(gathered.at[place], head_recv)

    def slot_at(dy):
        return ((y + dy) % y_count) * CORES + core

    def send_y(ref, dy, number):
        return remote(ref, ref, y_send.at[number], y_recv.at[number], device_at(0, dy, 0))

    def pass_core(index):
        remote(
            gathered.at[index], gathered.at[index], core_send, core_recv, device_at(0, 0, 1)
        ).start()

    own = gathered.at[place]
    if y_count == 8:
        halves = (pl.ds(0, 1), pl.ds(1, 1))
        far_low, far_high = (gathered.at[slot_at(4), half] for half in halves)
        first = [send_y(own, 2, 1), send_y(own, -2 + y_count, 3), send_y(own, 1, 0),
                 send_y(own, y_count - 1, 2)]
        for copy in first:
            copy.start()
        pass_core(place)
        below, above = gathered.at[slot_at(y_count - 2)], gathered.at[slot_at(2)]
        wait_bytes(below, y_recv.at[1])
        second = [send_y(gathered.at[slot_at(y_count - 2), halves[0]], 2, 6), send_y(below, 1, 4)]
        for copy in second:
            copy.start()
        wait_bytes(above, y_recv.at[3])
        third = [send_y(gathered.at[slot_at(2), halves[1]], y_count - 2, 7),
                 send_y(above, y_count - 1, 5)]
        for copy in third:
            copy.start()
        pass_core(slot_at(y_count - 2))
        pass_core(slot_at(2))
        for dy, number in ((y_count - 1, 0), (1, 2)):
            wait_bytes(gathered.at[slot_at(dy)], y_recv.at[number])
            pass_core(slot_at(dy))
        for dy, number in ((y_count - 3, 4), (3, 5)):
            wait_bytes(gathered.at[slot_at(dy)], y_recv.at[number])
            pass_core(slot_at(dy))
        wait_bytes(far_low, y_recv.at[6])
        wait_bytes(far_high, y_recv.at[7])
        pass_core(slot_at(4))
        y_copies = first + second + third
    else:
        y_copies = [send_y(own, dy, dy) for dy in range(1, y_count)]
        for copy in y_copies:
            copy.start()
        pass_core(place)
        for dy in range(1, y_count):
            wait_bytes(gathered.at[slot_at(y_count - dy)], y_recv.at[dy])
            pass_core(slot_at(y_count - dy))

    @pl.when((turn + last_step + 1) % 2 == 0)
    def _():
        for offset in range(x_count):
            ring_wait(last_step, offset)

    wait_bytes(gathered.at[pl.ds(0, y_count)], core_recv)

    half = gathered.shape[3] // 2
    rows = layer * 2 * half

    def project(owner):
        block = gathered[:, :, owner].astype(F32)
        left = jnp.concatenate(
            [block[:, :, :half].reshape(rows, -1), block[:, :, half:].reshape(rows, -1)], axis=1
        ).astype(BF16)
        right = jnp.concatenate([weights[owner, index] for index in range(x_count)], axis=1)
        return jnp.dot(left, right, preferred_element_type=F32)

    totals[...] = jnp.zeros_like(totals)

    def accumulate(owner, carry):
        product = project(owner)
        for dx in range(x_count):
            totals[dx * rows : (dx + 1) * rows, :] += product[:, dx * HDIM : (dx + 1) * HDIM]
        return carry

    lax.fori_loop(0, tensor_count // 2, accumulate, 0)
    for index in range(x_count):
        for column in range(2):
            for row in range(half):
                start = index * rows + column * half + row
                picked = totals[pl.ds(start, layer, stride=2 * half), :]
                out_send[index, column, row] = picked.astype(BF16)
    own_out = pltpu.make_async_copy(out_send.at[x], out_recv.at[x], out_recv_sem)
    own_out.start()
    for dx in range(1, x_count):
        remote(
            out_send.at[(x + dx) % x_count], out_recv.at[x], out_send_sem, out_recv_sem,
            device_at(dx, 0, 0),
        ).start()
    wait_bytes(out_recv, out_recv_sem)
    for index in range(x_count):
        pair, column = index // 2 * 2, index % 2
        both = out_recv[pair, column].astype(F32) + out_recv[pair + 1, column].astype(F32)
        out_ref[:, index * layer : (index + 1) * layer, :] = both.astype(BF16)

    wait_bytes(send.at[pl.ds(0, shard_count - 1)], query_send)
    wait_bytes(reply.at[pl.ds(0, shard_count - 1)], reply_send)
    for way, steps_sent in ((1, odd_steps), (0, even_steps)):
        if len(steps_sent):
            sent = weights.at[0, pl.ds(0, len(steps_sent))]
            pl.when(turn == way)(functools.partial(wait_bytes, sent, x_send))
    for step in range(last_step + 1):
        @pl.when((turn + step) % 2 == 0)
        def _():
            for offset in range(x_count):
                for down in ring_ways(step, offset):
                    ring_copy(down, step, offset).wait_send()
    wait_bytes(heads.at[pl.ds(0, tensor_count - 1)], head_send)
    pl.when(turn == 1)(functools.partial(wait_bytes, heads.at[0], head_send))
    for copy in y_copies:
        copy.wait_send()
    wait_bytes(gathered.at[pl.ds(0, y_count)], core_send)
    wait_bytes(out_send.at[pl.ds(0, x_count - 1)], out_send_sem)


def hand_on_kernel(self_in, out_in, self_out, out_out, sems):
    copies = [
        pltpu.make_async_copy(self_in, self_out, sems.at[0]),
        pltpu.make_async_copy(out_in, out_out, sems.at[1]),
    ]
    for copy in copies:
        copy.start()
    for copy in copies:
        copy.wait()


def on_device(
    self_query,
    cross_query,
    cache,
    step_kv,
    kv_length,
    positions,
    corpus_kv,
    neighbour_shard,
    neighbour_slot,
    out_weight,
):
    request_count, step_count, width = cross_query.shape
    head_count = width // HDIM
    shard_count = lax.axis_size("corpus")
    tensor_count = lax.axis_size("tensor")
    x_count, y_count = GRID_OF[shard_count]
    layer = y_count * CORES
    message_rows = head_count * 8
    row_count = request_count * step_count
    share = row_count // tensor_count
    smem = pl.BlockSpec(memory_space=pltpu.SMEM)
    vmem = pl.BlockSpec(memory_space=pltpu.VMEM)
    hbm = pl.BlockSpec(memory_space=pl.ANY)
    message = (shard_count, message_rows, HDIM)
    gather_shape = (layer, 2, tensor_count // 2, 2 * share, width // 2)
    out_shape = (share, shard_count, out_weight.shape[1])
    exchange = (x_count, 2, share, layer, out_weight.shape[1])
    dma = pltpu.SemaphoreType.DMA
    ring_shape = (2, max(1, tensor_count // 2), x_count)
    self_heads, cross_out = pl.pallas_call(
        main_kernel,
        out_shape=(
            jax.ShapeDtypeStruct(self_query.shape, BF16),
            jax.ShapeDtypeStruct(out_shape, BF16),
        ),
        in_specs=[hbm] * 2 + [smem] * 2 + [hbm] * 6,
        out_specs=(vmem, vmem),
        scratch_shapes=[
            pltpu.SMEM((2 * NBR, request_count), jnp.int32),
            pltpu.SMEM((2 * NBR, request_count), jnp.int32),
            pltpu.VMEM(cross_query.shape, BF16),
            pltpu.VMEM(self_query.shape, BF16),
            pltpu.VMEM(step_kv.shape, BF16),
            pltpu.VMEM((row_count, width), F32),
            pltpu.VMEM((2, row_count, width), F32),
            pltpu.VMEM((step_count, request_count, width), F32),
            pltpu.VMEM((2 * NBR * request_count, HDIM), jnp.int32),
            pltpu.VMEM((2 * NBR * request_count, HDIM), F32),
            pltpu.VMEM((shard_count * message_rows, HDIM), F32),
            pltpu.VMEM(cache.shape, BF16),
            pltpu.VMEM(corpus_kv.shape, BF16),
            pltpu.VMEM(message, BF16),
            pltpu.VMEM(message, BF16),
            pltpu.VMEM(message, BF16),
            pltpu.VMEM(message, BF16),
            pltpu.VMEM(message, F32),
            pltpu.VMEM(message, F32),
            pltpu.VMEM((tensor_count, 2 * share, width // 2), BF16),
            pltpu.VMEM(gather_shape, BF16),
            pltpu.VMEM((tensor_count // 2, x_count, width, HDIM), BF16),
            pltpu.VMEM((x_count * layer * 2 * share, HDIM), F32),
            pltpu.VMEM(exchange, BF16),
            pltpu.VMEM(exchange, BF16),
            pltpu.SemaphoreType.REGULAR,
            dma((8,)),
            dma, dma((x_count,)),
            dma, dma((x_count,)),
            dma, dma((x_count,)),
            dma(ring_shape), dma(ring_shape),
            dma, dma,
            dma((8,)), dma((8,)),
            dma, dma,
            dma, dma,
        ],
        compiler_params=pltpu.CompilerParams(
            collective_id=0, has_side_effects=True, vmem_limit_bytes=56 * 1024 * 1024
        ),
        name="retrieve_and_project",
    )(
        neighbour_shard.T, neighbour_slot.T, positions, kv_length,
        cross_query, self_query, step_kv, cache, corpus_kv, out_weight,
    )
    return pl.pallas_call(
        hand_on_kernel,
        out_shape=(
            jax.ShapeDtypeStruct(self_query.shape, BF16),
            jax.ShapeDtypeStruct(out_shape, BF16),
        ),
        in_specs=[vmem] * 2,
        out_specs=(hbm, hbm),
        scratch_shapes=[dma((2,))],
        name="hand_on",
    )(self_heads, cross_out)


def solution(mesh):
    return jax.shard_map(
        on_device,
        mesh=mesh,
        in_specs=(
            P("corpus", None, "tensor"),
            P("corpus", None, "tensor"),
            P("corpus", None, None, "tensor"),
            P("corpus", None, None, "tensor"),
            P("corpus"),
            P("corpus"),
            P("corpus", None, None, "tensor"),
            P("corpus", None),
            P("corpus", None),
            P("tensor", "corpus"),
        ),
        out_specs=(P("corpus", None, "tensor"), P("tensor", None, "corpus")),
        check_vma=False,
    )
```

```python
import functools

import jax
import jax.numpy as jnp
from jax import lax
from jax.experimental import pallas as pl
from jax.experimental.pallas import tpu as pltpu
from jax.sharding import PartitionSpec as P

HDIM = 128
NBR = 2
SPAN = 64
CORES = 2
GRID_OF = {64: (4, 8), 8: (2, 2)}
MESH = pl.DeviceIdType.MESH
masked_value = -1e30
F32 = jnp.float32
BF16 = jnp.bfloat16


def pack_queries(shards, slots, query, steps, columns, ranks, total, send_ref):
    item_count, request_count = shards.shape
    shard_count, message_rows, _ = send_ref.shape
    head_count = message_rows // 8
    count = item_count * request_count
    lane = lax.broadcasted_iota(jnp.int32, (1, HDIM), 1)
    shard_row = jnp.full((1, HDIM), -1, jnp.int32)
    tag_row = jnp.zeros((1, HDIM), jnp.int32)
    for number in range(count):
        item, request = divmod(number, request_count)
        shard = shards[item, request]
        shard_row = jnp.where(lane == number, shard, shard_row)
        tag_row = jnp.where(lane == number, slots[item, request] + 1, tag_row)
        columns[number : number + 1, :] = jnp.full((1, HDIM), shard, jnp.int32)
    same = columns[...] == shard_row
    here = lax.broadcasted_iota(jnp.int32, same.shape, 0)
    there = lax.broadcasted_iota(jnp.int32, same.shape, 1)
    ranks[...] = jnp.broadcast_to(
        jnp.sum(jnp.where(same & (there < here), 1.0, 0.0), axis=1, keepdims=True), same.shape
    )
    rank_row = jnp.sum(jnp.where(same & (here < there), 1.0, 0.0), axis=0, keepdims=True)
    for request in range(request_count):
        rows = query[request].astype(F32)
        for step in range(rows.shape[0]):
            steps[step, request : request + 1, :] = rows[step : step + 1, :]
    at_shard = shard_row == lax.broadcasted_iota(jnp.int32, (shard_count, HDIM), 0)
    for rank in range(2):
        chosen = jnp.where(at_shard & (rank_row == rank), 1.0, 0.0)
        tag = jnp.sum(chosen * tag_row.astype(F32), axis=1, keepdims=True)
        tag = jnp.broadcast_to(tag, (shard_count, HDIM))
        for head in range(head_count):
            total[pl.ds(head * 8 + 6 + rank, shard_count, stride=message_rows), :] = tag
        picker = chosen[:, :count].astype(BF16)
        for row in range(3):
            early, late = steps[row], steps[row + 1]
            items = jnp.concatenate([early] * NBR + [late] * NBR, axis=0).astype(BF16)
            packed = jnp.dot(picker, items, preferred_element_type=F32)
            for head in range(head_count):
                start = head * 8 + rank * 3 + row
                total[pl.ds(start, shard_count, stride=message_rows), :] = packed[
                    :, head * HDIM : (head + 1) * HDIM
                ]
    send_ref[...] = total[...].reshape(send_ref.shape).astype(BF16)


def attend_self(query_ref, fresh_ref, cached, length_ref, out_ref, heads):
    request_count, _, cache_length, _ = cached.shape
    row_count, width = query_ref.shape
    step_count = row_count // request_count
    key_count = request_count * cache_length
    row_request = lax.broadcasted_iota(jnp.int32, (row_count, key_count), 0) // step_count
    key_index = lax.broadcasted_iota(jnp.int32, (1, key_count), 1)
    limit = jnp.zeros((1, key_count), jnp.int32)
    for request in range(request_count):
        limit = jnp.where(key_index // cache_length == request, length_ref[request], limit)
    key_request = jnp.where(key_index % cache_length < limit, key_index // cache_length, -1)
    live = row_request == key_request
    fresh_row = lax.broadcasted_iota(jnp.int32, (row_count, row_count), 0)
    fresh_key = lax.broadcasted_iota(jnp.int32, (row_count, row_count), 1)
    fresh_live = (fresh_row // step_count == fresh_key // step_count) & (fresh_key <= fresh_row)
    scale = HDIM ** (-0.5)
    last = (((1,), (1,)), ((), ()))
    for head in heads:
        lanes = slice(head * HDIM, (head + 1) * HDIM)
        query = query_ref[:, lanes].astype(BF16)
        keys = cached[:, 0, :, lanes].reshape(key_count, HDIM)
        values = cached[:, 1, :, lanes].reshape(key_count, HDIM)
        scores = lax.dot_general(query, keys, last, preferred_element_type=F32) * scale
        scores = jnp.where(live, scores, masked_value)
        fresh = lax.dot_general(query, fresh_ref[0, :, lanes].astype(BF16), last, preferred_element_type=F32) * scale
        fresh = jnp.where(fresh_live, fresh, masked_value)
        top = jnp.maximum(
            jnp.max(scores, axis=1, keepdims=True), jnp.max(fresh, axis=1, keepdims=True)
        )
        weights = jnp.exp(scores - top)
        fresh_weights = jnp.exp(fresh - top)
        denom = jnp.sum(weights, axis=1, keepdims=True) + jnp.sum(fresh_weights, axis=1, keepdims=True)
        summed = jnp.dot(weights.astype(BF16), values, preferred_element_type=F32)
        summed = summed + jnp.dot(
            fresh_weights.astype(BF16), fresh_ref[1, :, lanes].astype(BF16), preferred_element_type=F32
        )
        result = summed / denom
        for request in range(request_count):
            rows = result[request * step_count : (request + 1) * step_count, :]
            out_ref[request, :, lanes] = rows.astype(BF16)


def attend_blocks(messages, blocks):
    source_count, message_rows, _ = messages.shape
    head_count = message_rows // 8
    block_count, _, token_count, _ = blocks.shape
    rows = source_count * 8
    scale = HDIM ** (-0.5)
    values = messages.astype(F32)
    in_tile = lax.broadcasted_iota(jnp.int32, (source_count, 8, HDIM), 1)
    lane = lax.broadcasted_iota(jnp.int32, (source_count, 8, HDIM), 2)
    tags = jnp.where(in_tile < 3, values[:, 6:7, :], values[:, 7:8, :]).reshape(rows, HDIM)
    tags = jnp.concatenate([tags, tags], axis=0)
    mine = [tags == F32(index + 1) for index in range(block_count)]
    kept = [jnp.where(entry, 1.0, 0.0).astype(BF16) for entry in mine]
    empty = jnp.zeros((rows, HDIM), F32)
    parts = []
    for head in range(0, head_count, 2):
        lanes = slice(head * HDIM, (head + 2) * HDIM)
        first, second = (
            values[:, entry * 8 : entry * 8 + 8, :].reshape(rows, HDIM) for entry in (head, head + 1)
        )
        query = jnp.concatenate(
            [
                jnp.concatenate([first, empty], axis=1),
                jnp.concatenate([empty, second], axis=1),
            ],
            axis=0,
        ).astype(BF16)
        chosen = jnp.zeros((2 * rows, token_count), F32)
        for index in range(0, block_count, 2):
            keys = blocks[index : index + 2, 0, :, lanes].reshape(2 * token_count, 2 * HDIM)
            scores = lax.dot_general(
                query, keys, (((1,), (1,)), ((), ())), preferred_element_type=F32
            )
            chosen = jnp.where(mine[index], scores[:, :token_count], chosen)
            chosen = jnp.where(mine[index + 1], scores[:, token_count:], chosen)
        chosen = chosen * scale
        top = jnp.max(chosen, axis=1, keepdims=True)
        weights = jnp.exp(chosen - top)
        denom = jnp.sum(weights, axis=1, keepdims=True)
        low_weights = weights.astype(BF16)
        spread = jnp.concatenate([low_weights * entry for entry in kept], axis=1)
        held = blocks[:, 1, :, lanes].reshape(block_count * token_count, 2 * HDIM)
        both = jnp.dot(spread, held, preferred_element_type=F32)
        summed = jnp.concatenate([both[:rows, :HDIM], both[rows:, HDIM:]], axis=0) / denom
        level = jnp.broadcast_to(top + jnp.log(denom), (2 * rows, HDIM))
        for entry in range(2):
            part = slice(entry * rows, (entry + 1) * rows)
            mean = summed[part].reshape(source_count, 8, HDIM)
            own = level[part].reshape(source_count, 8, HDIM)
            own = jnp.sum(jnp.where(lane % 8 == in_tile, own, 0.0), axis=1, keepdims=True)
            high = own.astype(BF16).astype(F32)
            middle = (own - high).astype(BF16).astype(F32)
            low = own - high - middle
            terms = jnp.where(lane < 8, high, jnp.where(lane < 16, middle, low))
            parts.append(jnp.where(in_tile == 6, terms, mean))
    return jnp.concatenate(parts, axis=1).astype(BF16)


def row_levels(values):
    source_count, message_rows, _ = values.shape
    tiles = values.reshape(source_count * message_rows // 8, 8, HDIM)
    in_tile = lax.broadcasted_iota(jnp.int32, tiles.shape, 1)
    lane = lax.broadcasted_iota(jnp.int32, tiles.shape, 2)
    terms = jnp.broadcast_to(tiles[:, 6:7, :], tiles.shape)
    picked = jnp.where((lane < 24) & (lane % 8 == in_tile), terms, 0.0)
    levels = jnp.sum(picked, axis=2, keepdims=True)
    return jnp.broadcast_to(levels, tiles.shape).reshape(values.shape)


def main_kernel(
    shard_ref, slot_ref, position_ref, length_ref,
    cross_ref, query_ref, fresh_ref, cache_ref, corpus_ref, weight_ref,
    self_ref, out_ref,
    shards, slots, cross, query, fresh, query_rows, fresh_rows, steps, columns, ranks, packed,
    cached, blocks, send, arrived, reply, returned, sums, levels,
    heads, gathered, weights, left, totals, out_send, out_recv,
    entered, local_sem, query_send, query_recv, reply_send, reply_recv,
    x_send, x_recv, ring_send, ring_recv, head_send, head_recv,
    y_send, y_recv, core_send, core_recv, out_send_sem, out_recv_sem,
):
    shard_count, message_rows, _ = send.shape
    x_count, y_count = GRID_OF[shard_count]
    layer = y_count * CORES
    tensor_count = heads.shape[0]
    request_count, step_count, _ = cross.shape
    me, mine = lax.axis_index("corpus"), lax.axis_index("tensor")
    x = me // layer
    y = (me // CORES) % y_count
    core = me % CORES
    turn = (x + mine) % 2

    def device_at(dx, dy, dc):
        return (((x + dx) % x_count) * y_count + (y + dy) % y_count) * CORES + (core + dc) % CORES

    def remote(source, target, send_sem, recv_sem, corpus=None, tensor=None):
        return pltpu.make_async_remote_copy(
            src_ref=source,
            dst_ref=target,
            send_sem=send_sem,
            recv_sem=recv_sem,
            device_id=(me if corpus is None else corpus, mine if tensor is None else tensor),
            device_id_type=MESH,
        )

    def wait_bytes(ref, sem):
        pltpu.make_async_copy(ref, ref, sem).wait()

    small = [
        pltpu.make_async_copy(source, target, local_sem.at[index])
        for index, (source, target) in enumerate(
            [(shard_ref, shards), (slot_ref, slots), (cross_ref, cross), (query_ref, query),
             (fresh_ref, fresh)]
        )
    ]
    for copy in small:
        copy.start()

    barrier = pltpu.get_barrier_semaphore()

    def greet(sem, corpus, tensor):
        pl.semaphore_signal(sem, inc=1, device_id=(corpus, tensor), device_id_type=MESH)

    for dx in range(1, x_count):
        greet(barrier, device_at(dx, 0, 0), mine)

    def greet_layer(step, carry):
        greet(barrier, device_at(0, step // CORES, step % CORES), mine)
        return carry

    def greet_tensor(step, carry):
        greet(barrier, me, (mine + step) % tensor_count)
        return carry

    lax.fori_loop(1, layer, greet_layer, 0)
    lax.fori_loop(1, tensor_count, greet_tensor, 0)
    own_place = weights.at[mine // 2, x]
    own_weight = pltpu.make_async_copy(weight_ref, own_place, local_sem.at[5])
    pl.when(turn == 0)(own_weight.start)
    cache_copy = pltpu.make_async_copy(cache_ref, cached, local_sem.at[6])
    corpus_copy = pltpu.make_async_copy(corpus_ref, blocks, local_sem.at[7])
    cache_copy.start()
    corpus_copy.start()
    pl.semaphore_wait(barrier, x_count - 1 + layer - 1 + tensor_count - 1)
    for dx in range(1, x_count):
        greet(entered, device_at(dx, 0, 0), mine)

    def send_weight(dx):
        remote(
            weight_ref, weights.at[mine // 2, x], x_send, x_recv.at[dx], device_at(dx, 0, 0)
        ).start()

    odd_steps, even_steps = range(1, x_count, 2), range(2, x_count, 2)

    @pl.when(turn == 1)
    def _():
        for dx in odd_steps:
            send_weight(dx)

    @pl.when(turn == 0)
    def _():
        for dx in even_steps:
            send_weight(dx)

    last_step, half_count = tensor_count // 2 - 1, x_count // 2

    def ring_copy(down, step, offset):
        owner = (mine + (step if down else tensor_count - step)) % tensor_count
        piece = weights.at[owner // 2, (x + offset) % x_count]
        after = (mine + (tensor_count - 1 if down else 1)) % tensor_count
        return remote(
            piece, piece, ring_send.at[down, step, offset], ring_recv.at[down, step, offset],
            tensor=after,
        )

    def ring_ways(step, offset):
        if step == last_step:
            return (0,) if offset < half_count else (1,)
        return (0, 1) if 0 <= step < last_step else ()

    def ring_wait(step, offset):
        for down in ring_ways(step, offset):
            ring_copy(down, step, offset).wait_recv()

    def ring_step(step, offset):
        if step > last_step:
            return

        @pl.when((turn + step) % 2 == 0)
        def _():
            ring_wait(step - 1, offset)
            for down in ring_ways(step, offset):
                ring_copy(down, step, offset).start()

    pl.when(turn == 0)(own_weight.wait)
    ring_step(0, 0)
    for copy in small:
        copy.wait()
    pack_queries(shards, slots, cross, steps, columns, ranks, packed, send)
    own_query = pltpu.make_async_copy(send.at[me], arrived.at[me], query_recv.at[0])
    own_query.start()
    ring_step(1, 0)
    pl.semaphore_wait(entered, x_count - 1)

    def both_cores(dx, dy):
        row = (((x + dx) % x_count) * y_count + (y + dy) % y_count) * CORES
        return row + core, row + 1 - core

    def send_query(target, dx):
        remote(send.at[target], arrived.at[me], query_send, query_recv.at[dx], target).start()

    def send_queries(dx, first):
        def body(dy, carry):
            for target in both_cores(dx, dy):
                send_query(target, dx)
            return carry

        if first:
            send_query(both_cores(0, 0)[1], 0)
        lax.fori_loop(first, y_count, body, 0)

    for dx in range(x_count):
        send_queries(dx, 1 if dx == 0 else 0)

    for request in range(request_count):
        rows = slice(request * step_count, (request + 1) * step_count)
        query_rows[rows, :] = query[request].astype(F32)
        for index in range(2):
            fresh_rows[index, rows, :] = fresh[request, index].astype(F32)
    cache_copy.wait()
    all_heads = range(message_rows // 8)

    for offset in range(1, x_count):
        @pl.when(turn == 0)
        def _():
            source = weights.at[mine // 2, (x + offset) % x_count]
            wait_bytes(source, x_recv.at[x_count - offset])

        ring_step(0, offset)
    attend_self(query_rows, fresh_rows, cached, length_ref, self_ref, all_heads[:2])
    ring_step(2, 0)
    attend_self(query_rows, fresh_rows, cached, length_ref, self_ref, all_heads[2:])
    corpus_copy.wait()

    def serve(dx, carry):
        first = pl.multiple_of(((x - dx + x_count) % x_count) * layer, layer)
        chunk = pl.ds(first, layer)
        wait_bytes(arrived.at[chunk], query_recv.at[dx])
        reply[chunk] = attend_blocks(arrived[chunk], blocks)

        def send_reply(target):
            remote(
                reply.at[target], returned.at[me], reply_send, reply_recv.at[dx], target
            ).start()

        def answer(dy, inner):
            for target in both_cores(x_count - dx, dy):
                send_reply(target)
            return inner

        pl.when(dx == 0)(lambda: send_reply(both_cores(0, 0)[1]))
        lax.fori_loop(jnp.where(dx == 0, 1, 0), y_count, answer, 0)
        if last_step > 0:
            for index, (step, offset) in enumerate(((1, 1), (1, 2), (1, 3), (2, 1))):
                pl.when(dx == index)(functools.partial(ring_step, step, offset))
        return carry

    lax.fori_loop(0, x_count, serve, 0)
    own_reply = pltpu.make_async_copy(reply.at[me], returned.at[me], reply_recv.at[0])
    own_reply.start()
    ring_step(2, 2)

    def decode(dx, carry):
        first = pl.multiple_of(((x + dx) % x_count) * layer, layer)
        chunk = pl.ds(first, layer)
        wait_bytes(returned.at[chunk], reply_recv.at[dx])
        values = returned[chunk].astype(F32)
        sums[chunk] = values
        levels[chunk] = row_levels(values)
        if last_step > 1:
            for index, (step, offset) in ((0, (2, 3)), (1, (3, 0)), (2, (3, 1))):
                pl.when(dx == index)(functools.partial(ring_step, step, offset))
        return carry

    lax.fori_loop(0, x_count, decode, 0)

    tile_row = lax.broadcasted_iota(jnp.int32, (message_rows, HDIM), 0) % 8

    def combined(request):
        boundary = SPAN - position_ref[request] % SPAN
        late = tile_row >= boundary

        def item(ref, number):
            tile = ref[shards[number, request]]
            second = ranks[pl.ds(number * request_count + request, 1), :] == 1.0
            if number < NBR:
                return jnp.where(second, pltpu.roll(tile, message_rows - 3, 0), tile)
            return jnp.where(
                second, pltpu.roll(tile, message_rows - 2, 0), pltpu.roll(tile, 1, 0)
            )

        def pair(ref):
            return [
                jnp.where(late, item(ref, NBR + number), item(ref, number)) for number in range(NBR)
            ]

        held, level = pair(sums), pair(levels)
        joint = jnp.maximum(level[0], level[1])
        factors = [jnp.exp(entry - joint) for entry in level]
        return (factors[0] * held[0] + factors[1] * held[1]) / (factors[0] + factors[1])

    def combine(owner):
        first = combined(owner * 2)
        second = pltpu.roll(combined(owner * 2 + 1), 4, 0)
        both = jnp.where(tile_row < 4, first, second)
        upper = jnp.concatenate([both[0:8], both[8:16]], axis=1)
        lower = jnp.concatenate([both[16:24], both[24:32]], axis=1)
        heads[owner] = jnp.concatenate([upper, lower], axis=0).astype(BF16)


    place = y * CORES + core
    taker = device_at(jnp.where(x % 2 == 0, turn, x_count - turn), 0, 0)

    def head_copy(owner):
        return remote(
            heads.at[owner], gathered.at[place, x % 2, mine // 2], head_send, head_recv,
            taker, owner,
        )

    own_heads = pltpu.make_async_copy(
        heads.at[mine], gathered.at[place, x % 2, mine // 2], head_recv
    )

    def send_heads(step, carry):
        owner = (mine + step) % tensor_count
        combine(owner)
        head_copy(owner).start()
        return carry

    lax.fori_loop(1, tensor_count, send_heads, 0)
    combine(mine)
    pl.when(turn == 0)(own_heads.start)

    @pl.when(turn == 1)
    def _():
        head_copy(mine).start()

    ring_step(3, 2)
    wait_bytes(gathered.at[place], head_recv)

    def slot_at(dy):
        return ((y + dy) % y_count) * CORES + core

    def send_y(ref, dy, number):
        return remote(ref, ref, y_send.at[number], y_recv.at[number], device_at(0, dy, 0))

    def pass_core(index):
        remote(
            gathered.at[index], gathered.at[index], core_send, core_recv, device_at(0, 0, 1)
        ).start()

    own = gathered.at[place]
    if y_count == 8:
        up, down = 1, y_count - 1

        def half_of(index, number):
            return gathered.at[index, pl.ds(number, 1)]

        y_copies = []

        def start_y(ref, dy, number):
            copy = send_y(ref, dy, number)
            copy.start()
            y_copies.append(copy)

        for number in range(2):
            start_y(half_of(place, number), 2, 2 + number)
            start_y(half_of(place, 1 - number), y_count - 2, 5 - number)
        start_y(own, up, 0)
        start_y(own, down, 1)
        pass_core(place)
        ring_step(3, 3)
        below, above = slot_at(y_count - 2), slot_at(2)
        for number in range(2):
            low_half, high_half = half_of(below, number), half_of(above, 1 - number)
            wait_bytes(low_half, y_recv.at[2 + number])
            if number == 0:
                start_y(low_half, 2, 10)
            start_y(low_half, up, 6 + number)
            wait_bytes(high_half, y_recv.at[5 - number])
            if number == 0:
                start_y(high_half, y_count - 2, 11)
            start_y(high_half, down, 9 - number)
        pass_core(below)
        pass_core(above)
        for dy, number in ((down, 0), (up, 1)):
            wait_bytes(gathered.at[slot_at(dy)], y_recv.at[number])
            pass_core(slot_at(dy))
        for dy, number in ((y_count - 3, 6), (3, 8)):
            for part in range(2):
                wait_bytes(half_of(slot_at(dy), part), y_recv.at[number + part])
            pass_core(slot_at(dy))
        wait_bytes(half_of(slot_at(4), 0), y_recv.at[10])
        wait_bytes(half_of(slot_at(4), 1), y_recv.at[11])
        pass_core(slot_at(4))
    else:
        y_copies = [send_y(own, dy, dy) for dy in range(1, y_count)]
        for copy in y_copies:
            copy.start()
        pass_core(place)
        for dy in range(1, y_count):
            wait_bytes(gathered.at[slot_at(y_count - dy)], y_recv.at[dy])
            pass_core(slot_at(y_count - dy))

    @pl.when((turn + last_step + 1) % 2 == 0)
    def _():
        for offset in range(x_count):
            ring_wait(last_step, offset)

    wait_bytes(gathered.at[pl.ds(0, y_count)], core_recv)

    half = gathered.shape[3] // 2
    rows = layer * 2 * half

    features = weights.shape[2]
    for owner in range(tensor_count // 2):
        block = gathered[:, :, owner].astype(F32)
        left[:, owner * features : (owner + 1) * features] = jnp.concatenate(
            [block[:, :, :half].reshape(rows, -1), block[:, :, half:].reshape(rows, -1)], axis=1
        ).astype(BF16)

    def send_out(dx):
        target = (x + dx) % x_count
        if dx == 0:
            pltpu.make_async_copy(out_send.at[x], out_recv.at[x], out_recv_sem).start()
        else:
            remote(
                out_send.at[target], out_recv.at[x], out_send_sem, out_recv_sem,
                device_at(dx, 0, 0),
            ).start()

    far_first = sorted(range(x_count), key=lambda dx: -min(dx, x_count - dx))
    for first in range(0, x_count, 2):
        group = far_first[first : first + 2]
        product = None
        for owner in range(tensor_count // 2):
            right = jnp.concatenate(
                [weights[owner, (x + dx) % x_count] for dx in group], axis=1
            )
            term = jnp.dot(
                left[:, owner * features : (owner + 1) * features], right,
                preferred_element_type=F32,
            )
            product = term if product is None else product + term
        for index, dx in enumerate(group):
            totals[...] = product[:, index * HDIM : (index + 1) * HDIM]
            for column in range(2):
                for row in range(half):
                    picked = totals[pl.ds(column * half + row, layer, stride=2 * half), :]
                    out_send[(x + dx) % x_count, column, row] = picked.astype(BF16)
            send_out(dx)
    wait_bytes(out_recv, out_recv_sem)
    for index in range(x_count):
        pair, column = index // 2 * 2, index % 2
        both = out_recv[pair, column].astype(F32) + out_recv[pair + 1, column].astype(F32)
        out_ref[:, index * layer : (index + 1) * layer, :] = both.astype(BF16)

    wait_bytes(send.at[pl.ds(0, shard_count - 1)], query_send)
    wait_bytes(reply.at[pl.ds(0, shard_count - 1)], reply_send)
    for way, steps_sent in ((1, odd_steps), (0, even_steps)):
        if len(steps_sent):
            sent = weights.at[0, pl.ds(0, len(steps_sent))]
            pl.when(turn == way)(functools.partial(wait_bytes, sent, x_send))
    for step in range(last_step + 1):
        @pl.when((turn + step) % 2 == 0)
        def _():
            for offset in range(x_count):
                for down in ring_ways(step, offset):
                    ring_copy(down, step, offset).wait_send()
    wait_bytes(heads.at[pl.ds(0, tensor_count - 1)], head_send)
    pl.when(turn == 1)(functools.partial(wait_bytes, heads.at[0], head_send))
    for copy in y_copies:
        copy.wait_send()
    wait_bytes(gathered.at[pl.ds(0, y_count)], core_send)
    wait_bytes(out_send.at[pl.ds(0, x_count - 1)], out_send_sem)


def hand_on_kernel(self_in, out_in, self_out, out_out, sems):
    copies = [
        pltpu.make_async_copy(self_in, self_out, sems.at[0]),
        pltpu.make_async_copy(out_in, out_out, sems.at[1]),
    ]
    for copy in copies:
        copy.start()
    for copy in copies:
        copy.wait()


def on_device(
    self_query,
    cross_query,
    cache,
    step_kv,
    kv_length,
    positions,
    corpus_kv,
    neighbour_shard,
    neighbour_slot,
    out_weight,
):
    request_count, step_count, width = cross_query.shape
    head_count = width // HDIM
    shard_count = lax.axis_size("corpus")
    tensor_count = lax.axis_size("tensor")
    x_count, y_count = GRID_OF[shard_count]
    layer = y_count * CORES
    message_rows = head_count * 8
    row_count = request_count * step_count
    share = row_count // tensor_count
    smem = pl.BlockSpec(memory_space=pltpu.SMEM)
    vmem = pl.BlockSpec(memory_space=pltpu.VMEM)
    hbm = pl.BlockSpec(memory_space=pl.ANY)
    message = (shard_count, message_rows, HDIM)
    gather_shape = (layer, 2, tensor_count // 2, 2 * share, width // 2)
    out_shape = (share, shard_count, out_weight.shape[1])
    exchange = (x_count, 2, share, layer, out_weight.shape[1])
    dma = pltpu.SemaphoreType.DMA
    ring_shape = (2, max(1, tensor_count // 2), x_count)
    self_heads, cross_out = pl.pallas_call(
        main_kernel,
        out_shape=(
            jax.ShapeDtypeStruct(self_query.shape, BF16),
            jax.ShapeDtypeStruct(out_shape, BF16),
        ),
        in_specs=[hbm] * 2 + [smem] * 2 + [hbm] * 6,
        out_specs=(vmem, vmem),
        scratch_shapes=[
            pltpu.SMEM((2 * NBR, request_count), jnp.int32),
            pltpu.SMEM((2 * NBR, request_count), jnp.int32),
            pltpu.VMEM(cross_query.shape, BF16),
            pltpu.VMEM(self_query.shape, BF16),
            pltpu.VMEM(step_kv.shape, BF16),
            pltpu.VMEM((row_count, width), F32),
            pltpu.VMEM((2, row_count, width), F32),
            pltpu.VMEM((step_count, request_count, width), F32),
            pltpu.VMEM((2 * NBR * request_count, HDIM), jnp.int32),
            pltpu.VMEM((2 * NBR * request_count, HDIM), F32),
            pltpu.VMEM((shard_count * message_rows, HDIM), F32),
            pltpu.VMEM(cache.shape, BF16),
            pltpu.VMEM(corpus_kv.shape, BF16),
            pltpu.VMEM(message, BF16),
            pltpu.VMEM(message, BF16),
            pltpu.VMEM(message, BF16),
            pltpu.VMEM(message, BF16),
            pltpu.VMEM(message, F32),
            pltpu.VMEM(message, F32),
            pltpu.VMEM((tensor_count, 2 * share, width // 2), BF16),
            pltpu.VMEM(gather_shape, BF16),
            pltpu.VMEM((tensor_count // 2, x_count, width, HDIM), BF16),
            pltpu.VMEM((layer * 2 * share, tensor_count // 2 * width), BF16),
            pltpu.VMEM((layer * 2 * share, HDIM), F32),
            pltpu.VMEM(exchange, BF16),
            pltpu.VMEM(exchange, BF16),
            pltpu.SemaphoreType.REGULAR,
            dma((8,)),
            dma, dma((x_count,)),
            dma, dma((x_count,)),
            dma, dma((x_count,)),
            dma(ring_shape), dma(ring_shape),
            dma, dma,
            dma((12,)), dma((12,)),
            dma, dma,
            dma, dma,
        ],
        compiler_params=pltpu.CompilerParams(
            collective_id=0, has_side_effects=True, vmem_limit_bytes=56 * 1024 * 1024
        ),
        name="retrieve_and_project",
    )(
        neighbour_shard.T, neighbour_slot.T, positions, kv_length,
        cross_query, self_query, step_kv, cache, corpus_kv, out_weight,
    )
    return pl.pallas_call(
        hand_on_kernel,
        out_shape=(
            jax.ShapeDtypeStruct(self_query.shape, BF16),
            jax.ShapeDtypeStruct(out_shape, BF16),
        ),
        in_specs=[vmem] * 2,
        out_specs=(hbm, hbm),
        scratch_shapes=[dma((2,))],
        name="hand_on",
    )(self_heads, cross_out)


def solution(mesh):
    return jax.shard_map(
        on_device,
        mesh=mesh,
        in_specs=(
            P("corpus", None, "tensor"),
            P("corpus", None, "tensor"),
            P("corpus", None, None, "tensor"),
            P("corpus", None, None, "tensor"),
            P("corpus"),
            P("corpus"),
            P("corpus", None, None, "tensor"),
            P("corpus", None),
            P("corpus", None),
            P("tensor", "corpus"),
        ),
        out_specs=(P("corpus", None, "tensor"), P("tensor", None, "corpus")),
        check_vma=False,
    )
```

```python
import functools

import jax
import jax.numpy as jnp
from jax import lax
from jax.experimental import pallas as pl
from jax.experimental.pallas import tpu as pltpu
from jax.sharding import PartitionSpec as P

HDIM = 128
NBR = 2
SPAN = 64
CORES = 2
GRID_OF = {64: (4, 8), 8: (2, 2)}
MESH = pl.DeviceIdType.MESH
masked_value = -1e30
F32 = jnp.float32
BF16 = jnp.bfloat16


def pack_queries(shards, slots, query, steps, columns, ranks, total, send_ref):
    item_count, request_count = shards.shape
    shard_count, message_rows, _ = send_ref.shape
    head_count = message_rows // 8
    count = item_count * request_count
    lane = lax.broadcasted_iota(jnp.int32, (1, HDIM), 1)
    shard_row = jnp.full((1, HDIM), -1, jnp.int32)
    tag_row = jnp.zeros((1, HDIM), jnp.int32)
    for number in range(count):
        item, request = divmod(number, request_count)
        shard = shards[item, request]
        shard_row = jnp.where(lane == number, shard, shard_row)
        tag_row = jnp.where(lane == number, slots[item, request] + 1, tag_row)
        columns[number : number + 1, :] = jnp.full((1, HDIM), shard, jnp.int32)
    same = columns[...] == shard_row
    here = lax.broadcasted_iota(jnp.int32, same.shape, 0)
    there = lax.broadcasted_iota(jnp.int32, same.shape, 1)
    ranks[...] = jnp.broadcast_to(
        jnp.sum(jnp.where(same & (there < here), 1.0, 0.0), axis=1, keepdims=True), same.shape
    )
    rank_row = jnp.sum(jnp.where(same & (here < there), 1.0, 0.0), axis=0, keepdims=True)
    for request in range(request_count):
        rows = query[request].astype(F32)
        for step in range(rows.shape[0]):
            steps[step, request : request + 1, :] = rows[step : step + 1, :]
    at_shard = shard_row == lax.broadcasted_iota(jnp.int32, (shard_count, HDIM), 0)
    for rank in range(2):
        chosen = jnp.where(at_shard & (rank_row == rank), 1.0, 0.0)
        tag = jnp.sum(chosen * tag_row.astype(F32), axis=1, keepdims=True)
        tag = jnp.broadcast_to(tag, (shard_count, HDIM))
        for head in range(head_count):
            total[pl.ds(head * 8 + 6 + rank, shard_count, stride=message_rows), :] = tag
        picker = chosen[:, :count].astype(BF16)
        for row in range(3):
            early, late = steps[row], steps[row + 1]
            items = jnp.concatenate([early] * NBR + [late] * NBR, axis=0).astype(BF16)
            packed = jnp.dot(picker, items, preferred_element_type=F32)
            for head in range(head_count):
                start = head * 8 + rank * 3 + row
                total[pl.ds(start, shard_count, stride=message_rows), :] = packed[
                    :, head * HDIM : (head + 1) * HDIM
                ]
    send_ref[...] = total[...].reshape(send_ref.shape).astype(BF16)


def attend_self(query_ref, fresh_ref, cached, length_ref, out_ref, heads):
    request_count, _, cache_length, _ = cached.shape
    row_count, width = query_ref.shape
    step_count = row_count // request_count
    key_count = request_count * cache_length
    row_request = lax.broadcasted_iota(jnp.int32, (row_count, key_count), 0) // step_count
    key_index = lax.broadcasted_iota(jnp.int32, (1, key_count), 1)
    limit = jnp.zeros((1, key_count), jnp.int32)
    for request in range(request_count):
        limit = jnp.where(key_index // cache_length == request, length_ref[request], limit)
    key_request = jnp.where(key_index % cache_length < limit, key_index // cache_length, -1)
    live = row_request == key_request
    fresh_row = lax.broadcasted_iota(jnp.int32, (row_count, row_count), 0)
    fresh_key = lax.broadcasted_iota(jnp.int32, (row_count, row_count), 1)
    fresh_live = (fresh_row // step_count == fresh_key // step_count) & (fresh_key <= fresh_row)
    scale = HDIM ** (-0.5)
    last = (((1,), (1,)), ((), ()))
    for head in heads:
        lanes = slice(head * HDIM, (head + 1) * HDIM)
        query = query_ref[:, lanes].astype(BF16)
        keys = cached[:, 0, :, lanes].reshape(key_count, HDIM)
        values = cached[:, 1, :, lanes].reshape(key_count, HDIM)
        scores = lax.dot_general(query, keys, last, preferred_element_type=F32) * scale
        scores = jnp.where(live, scores, masked_value)
        fresh = lax.dot_general(query, fresh_ref[0, :, lanes].astype(BF16), last, preferred_element_type=F32) * scale
        fresh = jnp.where(fresh_live, fresh, masked_value)
        top = jnp.maximum(
            jnp.max(scores, axis=1, keepdims=True), jnp.max(fresh, axis=1, keepdims=True)
        )
        weights = jnp.exp(scores - top)
        fresh_weights = jnp.exp(fresh - top)
        denom = jnp.sum(weights, axis=1, keepdims=True) + jnp.sum(fresh_weights, axis=1, keepdims=True)
        summed = jnp.dot(weights.astype(BF16), values, preferred_element_type=F32)
        summed = summed + jnp.dot(
            fresh_weights.astype(BF16), fresh_ref[1, :, lanes].astype(BF16), preferred_element_type=F32
        )
        result = summed / denom
        for request in range(request_count):
            rows = result[request * step_count : (request + 1) * step_count, :]
            out_ref[request, :, lanes] = rows.astype(BF16)


def attend_blocks(messages, blocks):
    source_count, message_rows, _ = messages.shape
    head_count = message_rows // 8
    block_count, _, token_count, _ = blocks.shape
    rows = source_count * 8
    scale = HDIM ** (-0.5)
    values = messages.astype(F32)
    in_tile = lax.broadcasted_iota(jnp.int32, (source_count, 8, HDIM), 1)
    lane = lax.broadcasted_iota(jnp.int32, (source_count, 8, HDIM), 2)
    tags = jnp.where(in_tile < 3, values[:, 6:7, :], values[:, 7:8, :]).reshape(rows, HDIM)
    tags = jnp.concatenate([tags, tags], axis=0)
    mine = [tags == F32(index + 1) for index in range(block_count)]
    kept = [jnp.where(entry, 1.0, 0.0).astype(BF16) for entry in mine]
    empty = jnp.zeros((rows, HDIM), F32)
    parts = []
    for head in range(0, head_count, 2):
        lanes = slice(head * HDIM, (head + 2) * HDIM)
        first, second = (
            values[:, entry * 8 : entry * 8 + 8, :].reshape(rows, HDIM) for entry in (head, head + 1)
        )
        query = jnp.concatenate(
            [
                jnp.concatenate([first, empty], axis=1),
                jnp.concatenate([empty, second], axis=1),
            ],
            axis=0,
        ).astype(BF16)
        chosen = jnp.zeros((2 * rows, token_count), F32)
        for index in range(0, block_count, 2):
            keys = blocks[index : index + 2, 0, :, lanes].reshape(2 * token_count, 2 * HDIM)
            scores = lax.dot_general(
                query, keys, (((1,), (1,)), ((), ())), preferred_element_type=F32
            )
            chosen = jnp.where(mine[index], scores[:, :token_count], chosen)
            chosen = jnp.where(mine[index + 1], scores[:, token_count:], chosen)
        chosen = chosen * scale
        top = jnp.max(chosen, axis=1, keepdims=True)
        weights = jnp.exp(chosen - top)
        denom = jnp.sum(weights, axis=1, keepdims=True)
        low_weights = weights.astype(BF16)
        spread = jnp.concatenate([low_weights * entry for entry in kept], axis=1)
        held = blocks[:, 1, :, lanes].reshape(block_count * token_count, 2 * HDIM)
        both = jnp.dot(spread, held, preferred_element_type=F32)
        summed = jnp.concatenate([both[:rows, :HDIM], both[rows:, HDIM:]], axis=0) / denom
        level = jnp.broadcast_to(top + jnp.log(denom), (2 * rows, HDIM))
        for entry in range(2):
            part = slice(entry * rows, (entry + 1) * rows)
            mean = summed[part].reshape(source_count, 8, HDIM)
            own = level[part].reshape(source_count, 8, HDIM)
            own = jnp.sum(jnp.where(lane % 8 == in_tile, own, 0.0), axis=1, keepdims=True)
            high = own.astype(BF16).astype(F32)
            middle = (own - high).astype(BF16).astype(F32)
            low = own - high - middle
            terms = jnp.where(lane < 8, high, jnp.where(lane < 16, middle, low))
            parts.append(jnp.where(in_tile == 6, terms, mean))
    return jnp.concatenate(parts, axis=1).astype(BF16)


def row_levels(values):
    source_count, message_rows, _ = values.shape
    tiles = values.reshape(source_count * message_rows // 8, 8, HDIM)
    in_tile = lax.broadcasted_iota(jnp.int32, tiles.shape, 1)
    lane = lax.broadcasted_iota(jnp.int32, tiles.shape, 2)
    terms = jnp.broadcast_to(tiles[:, 6:7, :], tiles.shape)
    picked = jnp.where((lane < 24) & (lane % 8 == in_tile), terms, 0.0)
    levels = jnp.sum(picked, axis=2, keepdims=True)
    return jnp.broadcast_to(levels, tiles.shape).reshape(values.shape)


def main_kernel(
    shard_ref, slot_ref, position_ref, length_ref,
    cross_ref, query_ref, fresh_ref, cache_ref, corpus_ref, weight_ref,
    self_ref, out_ref,
    shards, slots, cross, query, fresh, query_rows, fresh_rows, steps, columns, ranks, packed,
    cached, blocks, send, arrived, reply, returned, sums, levels,
    heads, gathered, weights, left, totals, out_send, out_recv,
    entered, local_sem, query_send, query_recv, reply_send, reply_recv,
    x_send, x_recv, ring_send, ring_recv, head_send, head_recv,
    y_send, y_recv, core_send, core_recv, out_send_sem, out_recv_sem,
):
    shard_count, message_rows, _ = send.shape
    x_count, y_count = GRID_OF[shard_count]
    layer = y_count * CORES
    tensor_count = heads.shape[0]
    request_count, step_count, _ = cross.shape
    me, mine = lax.axis_index("corpus"), lax.axis_index("tensor")
    x = me // layer
    y = (me // CORES) % y_count
    core = me % CORES
    turn = (x + mine) % 2

    def device_at(dx, dy, dc):
        return (((x + dx) % x_count) * y_count + (y + dy) % y_count) * CORES + (core + dc) % CORES

    def remote(source, target, send_sem, recv_sem, corpus=None, tensor=None):
        return pltpu.make_async_remote_copy(
            src_ref=source,
            dst_ref=target,
            send_sem=send_sem,
            recv_sem=recv_sem,
            device_id=(me if corpus is None else corpus, mine if tensor is None else tensor),
            device_id_type=MESH,
        )

    def wait_bytes(ref, sem):
        pltpu.make_async_copy(ref, ref, sem).wait()

    small = [
        pltpu.make_async_copy(source, target, local_sem.at[index])
        for index, (source, target) in enumerate(
            [(shard_ref, shards), (slot_ref, slots), (cross_ref, cross), (query_ref, query),
             (fresh_ref, fresh)]
        )
    ]
    for copy in small:
        copy.start()

    barrier = pltpu.get_barrier_semaphore()

    def greet(sem, corpus, tensor):
        pl.semaphore_signal(sem, inc=1, device_id=(corpus, tensor), device_id_type=MESH)

    for dx in range(1, x_count):
        greet(barrier, device_at(dx, 0, 0), mine)

    def greet_layer(step, carry):
        greet(barrier, device_at(0, step // CORES, step % CORES), mine)
        return carry

    def greet_tensor(step, carry):
        greet(barrier, me, (mine + step) % tensor_count)
        return carry

    lax.fori_loop(1, layer, greet_layer, 0)
    lax.fori_loop(1, tensor_count, greet_tensor, 0)
    own_place = weights.at[mine // 2, x]
    own_weight = pltpu.make_async_copy(weight_ref, own_place, local_sem.at[5])
    pl.when(turn == 0)(own_weight.start)
    cache_copy = pltpu.make_async_copy(cache_ref, cached, local_sem.at[6])
    corpus_copy = pltpu.make_async_copy(corpus_ref, blocks, local_sem.at[7])
    cache_copy.start()
    corpus_copy.start()
    pl.semaphore_wait(barrier, x_count - 1 + layer - 1 + tensor_count - 1)
    for dx in range(1, x_count):
        greet(entered, device_at(dx, 0, 0), mine)

    def send_weight(dx):
        remote(
            weight_ref, weights.at[mine // 2, x], x_send, x_recv.at[dx], device_at(dx, 0, 0)
        ).start()

    odd_steps, even_steps = range(1, x_count, 2), range(2, x_count, 2)

    @pl.when(turn == 1)
    def _():
        for dx in odd_steps:
            send_weight(dx)

    @pl.when(turn == 0)
    def _():
        for dx in even_steps:
            send_weight(dx)

    last_step, half_count = tensor_count // 2 - 1, x_count // 2

    def ring_copy(down, step, offset):
        owner = (mine + (step if down else tensor_count - step)) % tensor_count
        piece = weights.at[owner // 2, (x + offset) % x_count]
        after = (mine + (tensor_count - 1 if down else 1)) % tensor_count
        return remote(
            piece, piece, ring_send.at[down, step, offset], ring_recv.at[down, step, offset],
            tensor=after,
        )

    def ring_ways(step, offset):
        if step == last_step:
            return (0,) if offset < half_count else (1,)
        return (0, 1) if 0 <= step < last_step else ()

    def ring_wait(step, offset):
        for down in ring_ways(step, offset):
            ring_copy(down, step, offset).wait_recv()

    def ring_step(step, offset):
        if step > last_step:
            return

        @pl.when((turn + step) % 2 == 0)
        def _():
            ring_wait(step - 1, offset)
            for down in ring_ways(step, offset):
                ring_copy(down, step, offset).start()

    pl.when(turn == 0)(own_weight.wait)
    ring_step(0, 0)
    for copy in small:
        copy.wait()
    pack_queries(shards, slots, cross, steps, columns, ranks, packed, send)
    own_query = pltpu.make_async_copy(send.at[me], arrived.at[me], query_recv.at[0])
    own_query.start()
    ring_step(1, 0)

    def both_cores(dx, dy):
        row = (((x + dx) % x_count) * y_count + (y + dy) % y_count) * CORES
        return row + core, row + 1 - core

    def send_query(target, dx):
        remote(send.at[target], arrived.at[me], query_send, query_recv.at[dx], target).start()

    def send_queries(dx, first):
        def body(dy, carry):
            for target in both_cores(dx, dy):
                send_query(target, dx)
            return carry

        if first:
            send_query(both_cores(0, 0)[1], 0)
        lax.fori_loop(first, y_count, body, 0)

    send_queries(0, 1)
    pl.semaphore_wait(entered, x_count - 1)
    for dx in range(1, x_count):
        send_queries(dx, 0)

    for request in range(request_count):
        rows = slice(request * step_count, (request + 1) * step_count)
        query_rows[rows, :] = query[request].astype(F32)
        for index in range(2):
            fresh_rows[index, rows, :] = fresh[request, index].astype(F32)
    cache_copy.wait()
    all_heads = range(message_rows // 8)

    for offset in range(1, x_count):
        @pl.when(turn == 0)
        def _():
            source = weights.at[mine // 2, (x + offset) % x_count]
            wait_bytes(source, x_recv.at[x_count - offset])

        ring_step(0, offset)
    attend_self(query_rows, fresh_rows, cached, length_ref, self_ref, all_heads[:2])
    ring_step(2, 0)
    attend_self(query_rows, fresh_rows, cached, length_ref, self_ref, all_heads[2:])
    corpus_copy.wait()

    def serve(dx, carry):
        first = pl.multiple_of(((x - dx + x_count) % x_count) * layer, layer)
        chunk = pl.ds(first, layer)
        wait_bytes(arrived.at[chunk], query_recv.at[dx])
        reply[chunk] = attend_blocks(arrived[chunk], blocks)

        def send_reply(target):
            remote(
                reply.at[target], returned.at[me], reply_send, reply_recv.at[dx], target
            ).start()

        def answer(dy, inner):
            for target in both_cores(x_count - dx, dy):
                send_reply(target)
            return inner

        pl.when(dx == 0)(lambda: send_reply(both_cores(0, 0)[1]))
        lax.fori_loop(jnp.where(dx == 0, 1, 0), y_count, answer, 0)
        if last_step > 0:
            for index, (step, offset) in enumerate(((1, 1), (1, 2), (1, 3), (2, 1))):
                pl.when(dx == index)(functools.partial(ring_step, step, offset))
        return carry

    lax.fori_loop(0, x_count, serve, 0)
    own_reply = pltpu.make_async_copy(reply.at[me], returned.at[me], reply_recv.at[0])
    own_reply.start()
    ring_step(2, 2)

    def decode(dx, carry):
        first = pl.multiple_of(((x + dx) % x_count) * layer, layer)
        chunk = pl.ds(first, layer)
        wait_bytes(returned.at[chunk], reply_recv.at[dx])
        values = returned[chunk].astype(F32)
        sums[chunk] = values
        levels[chunk] = row_levels(values)
        if last_step > 1:
            for index, (step, offset) in ((0, (2, 3)),):
                pl.when(dx == index)(functools.partial(ring_step, step, offset))
        return carry

    lax.fori_loop(0, x_count, decode, 0)

    tile_row = lax.broadcasted_iota(jnp.int32, (message_rows, HDIM), 0) % 8

    def combined(request):
        boundary = SPAN - position_ref[request] % SPAN
        late = tile_row >= boundary

        def item(ref, number):
            tile = ref[shards[number, request]]
            second = ranks[pl.ds(number * request_count + request, 1), :] == 1.0
            if number < NBR:
                return jnp.where(second, pltpu.roll(tile, message_rows - 3, 0), tile)
            return jnp.where(
                second, pltpu.roll(tile, message_rows - 2, 0), pltpu.roll(tile, 1, 0)
            )

        def pair(ref):
            return [
                jnp.where(late, item(ref, NBR + number), item(ref, number)) for number in range(NBR)
            ]

        held, level = pair(sums), pair(levels)
        joint = jnp.maximum(level[0], level[1])
        factors = [jnp.exp(entry - joint) for entry in level]
        return (factors[0] * held[0] + factors[1] * held[1]) / (factors[0] + factors[1])

    def combine(owner):
        first = combined(owner * 2)
        second = pltpu.roll(combined(owner * 2 + 1), 4, 0)
        both = jnp.where(tile_row < 4, first, second)
        upper = jnp.concatenate([both[0:8], both[8:16]], axis=1)
        lower = jnp.concatenate([both[16:24], both[24:32]], axis=1)
        heads[owner] = jnp.concatenate([upper, lower], axis=0).astype(BF16)


    place = y * CORES + core
    taker = device_at(jnp.where(x % 2 == 0, turn, x_count - turn), 0, 0)

    def head_copy(owner):
        return remote(
            heads.at[owner], gathered.at[place, x % 2, mine // 2], head_send, head_recv,
            taker, owner,
        )

    own_heads = pltpu.make_async_copy(
        heads.at[mine], gathered.at[place, x % 2, mine // 2], head_recv
    )

    def send_heads(step, carry):
        owner = (mine + step) % tensor_count
        combine(owner)
        head_copy(owner).start()
        return carry

    lax.fori_loop(1, tensor_count, send_heads, 0)
    combine(mine)
    pl.when(turn == 0)(own_heads.start)

    @pl.when(turn == 1)
    def _():
        head_copy(mine).start()

    wait_bytes(gathered.at[place], head_recv)

    def slot_at(dy):
        return ((y + dy) % y_count) * CORES + core

    def send_y(ref, dy, number):
        return remote(ref, ref, y_send.at[number], y_recv.at[number], device_at(0, dy, 0))

    def pass_core(index):
        remote(
            gathered.at[index], gathered.at[index], core_send, core_recv, device_at(0, 0, 1)
        ).start()

    own = gathered.at[place]
    if y_count == 8:
        up, down = 1, y_count - 1

        def half_of(index, number):
            return gathered.at[index, pl.ds(number, 1)]

        y_copies = []

        def start_y(ref, dy, number):
            copy = send_y(ref, dy, number)
            copy.start()
            y_copies.append(copy)

        for number in range(2):
            start_y(half_of(place, number), 2, 2 + number)
            start_y(half_of(place, 1 - number), y_count - 2, 5 - number)
        start_y(own, up, 0)
        start_y(own, down, 1)
        pass_core(place)
        for offset in range(x_count):
            ring_step(3, offset)
        below, above = slot_at(y_count - 2), slot_at(2)
        for number in range(2):
            low_half, high_half = half_of(below, number), half_of(above, 1 - number)
            wait_bytes(low_half, y_recv.at[2 + number])
            if number == 0:
                start_y(low_half, 2, 10)
            start_y(low_half, up, 6 + number)
            wait_bytes(high_half, y_recv.at[5 - number])
            if number == 0:
                start_y(high_half, y_count - 2, 11)
            start_y(high_half, down, 9 - number)
        pass_core(below)
        pass_core(above)
        for dy, number in ((down, 0), (up, 1)):
            wait_bytes(gathered.at[slot_at(dy)], y_recv.at[number])
            pass_core(slot_at(dy))
        for dy, number in ((y_count - 3, 6), (3, 8)):
            for part in range(2):
                wait_bytes(half_of(slot_at(dy), part), y_recv.at[number + part])
            pass_core(slot_at(dy))
        wait_bytes(half_of(slot_at(4), 0), y_recv.at[10])
        wait_bytes(half_of(slot_at(4), 1), y_recv.at[11])
        pass_core(slot_at(4))
    else:
        y_copies = [send_y(own, dy, dy) for dy in range(1, y_count)]
        for copy in y_copies:
            copy.start()
        pass_core(place)
        for dy in range(1, y_count):
            wait_bytes(gathered.at[slot_at(y_count - dy)], y_recv.at[dy])
            pass_core(slot_at(y_count - dy))

    @pl.when((turn + last_step + 1) % 2 == 0)
    def _():
        for offset in range(x_count):
            ring_wait(last_step, offset)

    wait_bytes(gathered.at[pl.ds(0, y_count)], core_recv)

    half = gathered.shape[3] // 2
    rows = layer * 2 * half

    features = weights.shape[2]
    for owner in range(tensor_count // 2):
        block = gathered[:, :, owner].astype(F32)
        left[:, owner * features : (owner + 1) * features] = jnp.concatenate(
            [block[:, :, :half].reshape(rows, -1), block[:, :, half:].reshape(rows, -1)], axis=1
        ).astype(BF16)

    def send_out(dx):
        target = (x + dx) % x_count
        if dx == 0:
            pltpu.make_async_copy(out_send.at[x], out_recv.at[x], out_recv_sem).start()
        else:
            remote(
                out_send.at[target], out_recv.at[x], out_send_sem, out_recv_sem,
                device_at(dx, 0, 0),
            ).start()

    far_first = sorted(range(x_count), key=lambda dx: -min(dx, x_count - dx))
    for first in range(0, x_count, 2):
        group = far_first[first : first + 2]
        product = None
        for owner in range(tensor_count // 2):
            right = jnp.concatenate(
                [weights[owner, (x + dx) % x_count] for dx in group], axis=1
            )
            term = jnp.dot(
                left[:, owner * features : (owner + 1) * features], right,
                preferred_element_type=F32,
            )
            product = term if product is None else product + term
        for index, dx in enumerate(group):
            totals[...] = product[:, index * HDIM : (index + 1) * HDIM]
            for column in range(2):
                for row in range(half):
                    picked = totals[pl.ds(column * half + row, layer, stride=2 * half), :]
                    out_send[(x + dx) % x_count, column, row] = picked.astype(BF16)
            send_out(dx)
    wait_bytes(out_recv, out_recv_sem)
    for index in range(x_count):
        pair, column = index // 2 * 2, index % 2
        both = out_recv[pair, column].astype(F32) + out_recv[pair + 1, column].astype(F32)
        out_ref[:, index * layer : (index + 1) * layer, :] = both.astype(BF16)

    wait_bytes(send.at[pl.ds(0, shard_count - 1)], query_send)
    wait_bytes(reply.at[pl.ds(0, shard_count - 1)], reply_send)
    for way, steps_sent in ((1, odd_steps), (0, even_steps)):
        if len(steps_sent):
            sent = weights.at[0, pl.ds(0, len(steps_sent))]
            pl.when(turn == way)(functools.partial(wait_bytes, sent, x_send))
    for step in range(last_step + 1):
        @pl.when((turn + step) % 2 == 0)
        def _():
            for offset in range(x_count):
                for down in ring_ways(step, offset):
                    ring_copy(down, step, offset).wait_send()
    wait_bytes(heads.at[pl.ds(0, tensor_count - 1)], head_send)
    pl.when(turn == 1)(functools.partial(wait_bytes, heads.at[0], head_send))
    for copy in y_copies:
        copy.wait_send()
    wait_bytes(gathered.at[pl.ds(0, y_count)], core_send)
    wait_bytes(out_send.at[pl.ds(0, x_count - 1)], out_send_sem)


def hand_on_kernel(self_in, out_in, self_out, out_out, sems):
    copies = [
        pltpu.make_async_copy(self_in, self_out, sems.at[0]),
        pltpu.make_async_copy(out_in, out_out, sems.at[1]),
    ]
    for copy in copies:
        copy.start()
    for copy in copies:
        copy.wait()


def on_device(
    self_query,
    cross_query,
    cache,
    step_kv,
    kv_length,
    positions,
    corpus_kv,
    neighbour_shard,
    neighbour_slot,
    out_weight,
):
    request_count, step_count, width = cross_query.shape
    head_count = width // HDIM
    shard_count = lax.axis_size("corpus")
    tensor_count = lax.axis_size("tensor")
    x_count, y_count = GRID_OF[shard_count]
    layer = y_count * CORES
    message_rows = head_count * 8
    row_count = request_count * step_count
    share = row_count // tensor_count
    smem = pl.BlockSpec(memory_space=pltpu.SMEM)
    vmem = pl.BlockSpec(memory_space=pltpu.VMEM)
    hbm = pl.BlockSpec(memory_space=pl.ANY)
    message = (shard_count, message_rows, HDIM)
    gather_shape = (layer, 2, tensor_count // 2, 2 * share, width // 2)
    out_shape = (share, shard_count, out_weight.shape[1])
    exchange = (x_count, 2, share, layer, out_weight.shape[1])
    dma = pltpu.SemaphoreType.DMA
    ring_shape = (2, max(1, tensor_count // 2), x_count)
    self_heads, cross_out = pl.pallas_call(
        main_kernel,
        out_shape=(
            jax.ShapeDtypeStruct(self_query.shape, BF16),
            jax.ShapeDtypeStruct(out_shape, BF16),
        ),
        in_specs=[hbm] * 2 + [smem] * 2 + [hbm] * 6,
        out_specs=(vmem, vmem),
        scratch_shapes=[
            pltpu.SMEM((2 * NBR, request_count), jnp.int32),
            pltpu.SMEM((2 * NBR, request_count), jnp.int32),
            pltpu.VMEM(cross_query.shape, BF16),
            pltpu.VMEM(self_query.shape, BF16),
            pltpu.VMEM(step_kv.shape, BF16),
            pltpu.VMEM((row_count, width), F32),
            pltpu.VMEM((2, row_count, width), F32),
            pltpu.VMEM((step_count, request_count, width), F32),
            pltpu.VMEM((2 * NBR * request_count, HDIM), jnp.int32),
            pltpu.VMEM((2 * NBR * request_count, HDIM), F32),
            pltpu.VMEM((shard_count * message_rows, HDIM), F32),
            pltpu.VMEM(cache.shape, BF16),
            pltpu.VMEM(corpus_kv.shape, BF16),
            pltpu.VMEM(message, BF16),
            pltpu.VMEM(message, BF16),
            pltpu.VMEM(message, BF16),
            pltpu.VMEM(message, BF16),
            pltpu.VMEM(message, F32),
            pltpu.VMEM(message, F32),
            pltpu.VMEM((tensor_count, 2 * share, width // 2), BF16),
            pltpu.VMEM(gather_shape, BF16),
            pltpu.VMEM((tensor_count // 2, x_count, width, HDIM), BF16),
            pltpu.VMEM((layer * 2 * share, tensor_count // 2 * width), BF16),
            pltpu.VMEM((layer * 2 * share, HDIM), F32),
            pltpu.VMEM(exchange, BF16),
            pltpu.VMEM(exchange, BF16),
            pltpu.SemaphoreType.REGULAR,
            dma((8,)),
            dma, dma((x_count,)),
            dma, dma((x_count,)),
            dma, dma((x_count,)),
            dma(ring_shape), dma(ring_shape),
            dma, dma,
            dma((12,)), dma((12,)),
            dma, dma,
            dma, dma,
        ],
        compiler_params=pltpu.CompilerParams(
            collective_id=0, has_side_effects=True, vmem_limit_bytes=56 * 1024 * 1024
        ),
        name="retrieve_and_project",
    )(
        neighbour_shard.T, neighbour_slot.T, positions, kv_length,
        cross_query, self_query, step_kv, cache, corpus_kv, out_weight,
    )
    return pl.pallas_call(
        hand_on_kernel,
        out_shape=(
            jax.ShapeDtypeStruct(self_query.shape, BF16),
            jax.ShapeDtypeStruct(out_shape, BF16),
        ),
        in_specs=[vmem] * 2,
        out_specs=(hbm, hbm),
        scratch_shapes=[dma((2,))],
        name="hand_on",
    )(self_heads, cross_out)


def solution(mesh):
    return jax.shard_map(
        on_device,
        mesh=mesh,
        in_specs=(
            P("corpus", None, "tensor"),
            P("corpus", None, "tensor"),
            P("corpus", None, None, "tensor"),
            P("corpus", None, None, "tensor"),
            P("corpus"),
            P("corpus"),
            P("corpus", None, None, "tensor"),
            P("corpus", None),
            P("corpus", None),
            P("tensor", "corpus"),
        ),
        out_specs=(P("corpus", None, "tensor"), P("tensor", None, "corpus")),
        check_vma=False,
    )
```

```python
import functools

import jax
import jax.numpy as jnp
from jax import lax
from jax.experimental import pallas as pl
from jax.experimental.pallas import tpu as pltpu
from jax.sharding import PartitionSpec as P

HDIM = 128
NBR = 2
SPAN = 64
CORES = 2
GRID_OF = {64: (4, 8), 8: (2, 2)}
MESH = pl.DeviceIdType.MESH
masked_value = -1e30
F32 = jnp.float32
BF16 = jnp.bfloat16


def pack_queries(shards, slots, query, steps, columns, ranks, total, send_ref):
    item_count, request_count = shards.shape
    shard_count, message_rows, _ = send_ref.shape
    head_count = message_rows // 8
    count = item_count * request_count
    lane = lax.broadcasted_iota(jnp.int32, (1, HDIM), 1)
    shard_row = jnp.full((1, HDIM), -1, jnp.int32)
    tag_row = jnp.zeros((1, HDIM), jnp.int32)
    for number in range(count):
        item, request = divmod(number, request_count)
        shard = shards[item, request]
        shard_row = jnp.where(lane == number, shard, shard_row)
        tag_row = jnp.where(lane == number, slots[item, request] + 1, tag_row)
        columns[number : number + 1, :] = jnp.full((1, HDIM), shard, jnp.int32)
    same = columns[...] == shard_row
    here = lax.broadcasted_iota(jnp.int32, same.shape, 0)
    there = lax.broadcasted_iota(jnp.int32, same.shape, 1)
    ranks[...] = jnp.broadcast_to(
        jnp.sum(jnp.where(same & (there < here), 1.0, 0.0), axis=1, keepdims=True), same.shape
    )
    rank_row = jnp.sum(jnp.where(same & (here < there), 1.0, 0.0), axis=0, keepdims=True)
    for request in range(request_count):
        rows = query[request].astype(F32)
        for step in range(rows.shape[0]):
            steps[step, request : request + 1, :] = rows[step : step + 1, :]
    at_shard = shard_row == lax.broadcasted_iota(jnp.int32, (shard_count, HDIM), 0)
    for rank in range(2):
        chosen = jnp.where(at_shard & (rank_row == rank), 1.0, 0.0)
        tag = jnp.sum(chosen * tag_row.astype(F32), axis=1, keepdims=True)
        tag = jnp.broadcast_to(tag, (shard_count, HDIM))
        for head in range(head_count):
            total[pl.ds(head * 8 + 6 + rank, shard_count, stride=message_rows), :] = tag
        picker = chosen[:, :count].astype(BF16)
        for row in range(3):
            early, late = steps[row], steps[row + 1]
            items = jnp.concatenate([early] * NBR + [late] * NBR, axis=0).astype(BF16)
            packed = jnp.dot(picker, items, preferred_element_type=F32)
            for head in range(head_count):
                start = head * 8 + rank * 3 + row
                total[pl.ds(start, shard_count, stride=message_rows), :] = packed[
                    :, head * HDIM : (head + 1) * HDIM
                ]
    send_ref[...] = total[...].reshape(send_ref.shape).astype(BF16)


def attend_self(query_ref, fresh_ref, cached, length_ref, out_ref, heads):
    request_count, _, cache_length, _ = cached.shape
    row_count, width = query_ref.shape
    step_count = row_count // request_count
    key_count = request_count * cache_length
    row_request = lax.broadcasted_iota(jnp.int32, (row_count, key_count), 0) // step_count
    key_index = lax.broadcasted_iota(jnp.int32, (1, key_count), 1)
    limit = jnp.zeros((1, key_count), jnp.int32)
    for request in range(request_count):
        limit = jnp.where(key_index // cache_length == request, length_ref[request], limit)
    key_request = jnp.where(key_index % cache_length < limit, key_index // cache_length, -1)
    live = row_request == key_request
    fresh_row = lax.broadcasted_iota(jnp.int32, (row_count, row_count), 0)
    fresh_key = lax.broadcasted_iota(jnp.int32, (row_count, row_count), 1)
    fresh_live = (fresh_row // step_count == fresh_key // step_count) & (fresh_key <= fresh_row)
    scale = HDIM ** (-0.5)
    last = (((1,), (1,)), ((), ()))
    for head in heads:
        lanes = slice(head * HDIM, (head + 1) * HDIM)
        query = query_ref[:, lanes].astype(BF16)
        keys = cached[:, 0, :, lanes].reshape(key_count, HDIM)
        values = cached[:, 1, :, lanes].reshape(key_count, HDIM)
        scores = lax.dot_general(query, keys, last, preferred_element_type=F32) * scale
        scores = jnp.where(live, scores, masked_value)
        fresh = lax.dot_general(query, fresh_ref[0, :, lanes].astype(BF16), last, preferred_element_type=F32) * scale
        fresh = jnp.where(fresh_live, fresh, masked_value)
        top = jnp.maximum(
            jnp.max(scores, axis=1, keepdims=True), jnp.max(fresh, axis=1, keepdims=True)
        )
        weights = jnp.exp(scores - top)
        fresh_weights = jnp.exp(fresh - top)
        denom = jnp.sum(weights, axis=1, keepdims=True) + jnp.sum(fresh_weights, axis=1, keepdims=True)
        summed = jnp.dot(weights.astype(BF16), values, preferred_element_type=F32)
        summed = summed + jnp.dot(
            fresh_weights.astype(BF16), fresh_ref[1, :, lanes].astype(BF16), preferred_element_type=F32
        )
        result = summed / denom
        for request in range(request_count):
            rows = result[request * step_count : (request + 1) * step_count, :]
            out_ref[request, :, lanes] = rows.astype(BF16)


def attend_blocks(messages, blocks):
    source_count, message_rows, _ = messages.shape
    head_count = message_rows // 8
    block_count, _, token_count, _ = blocks.shape
    rows = source_count * 8
    scale = HDIM ** (-0.5)
    values = messages.astype(F32)
    in_tile = lax.broadcasted_iota(jnp.int32, (source_count, 8, HDIM), 1)
    lane = lax.broadcasted_iota(jnp.int32, (source_count, 8, HDIM), 2)
    tags = jnp.where(in_tile < 3, values[:, 6:7, :], values[:, 7:8, :]).reshape(rows, HDIM)
    tags = jnp.concatenate([tags, tags], axis=0)
    mine = [tags == F32(index + 1) for index in range(block_count)]
    kept = [jnp.where(entry, 1.0, 0.0).astype(BF16) for entry in mine]
    empty = jnp.zeros((rows, HDIM), F32)
    parts = []
    for head in range(0, head_count, 2):
        lanes = slice(head * HDIM, (head + 2) * HDIM)
        first, second = (
            values[:, entry * 8 : entry * 8 + 8, :].reshape(rows, HDIM) for entry in (head, head + 1)
        )
        query = jnp.concatenate(
            [
                jnp.concatenate([first, empty], axis=1),
                jnp.concatenate([empty, second], axis=1),
            ],
            axis=0,
        ).astype(BF16)
        chosen = jnp.zeros((2 * rows, token_count), F32)
        for index in range(0, block_count, 2):
            keys = blocks[index : index + 2, 0, :, lanes].reshape(2 * token_count, 2 * HDIM)
            scores = lax.dot_general(
                query, keys, (((1,), (1,)), ((), ())), preferred_element_type=F32
            )
            chosen = jnp.where(mine[index], scores[:, :token_count], chosen)
            chosen = jnp.where(mine[index + 1], scores[:, token_count:], chosen)
        chosen = chosen * scale
        top = jnp.max(chosen, axis=1, keepdims=True)
        weights = jnp.exp(chosen - top)
        denom = jnp.sum(weights, axis=1, keepdims=True)
        low_weights = weights.astype(BF16)
        spread = jnp.concatenate([low_weights * entry for entry in kept], axis=1)
        held = blocks[:, 1, :, lanes].reshape(block_count * token_count, 2 * HDIM)
        both = jnp.dot(spread, held, preferred_element_type=F32)
        summed = jnp.concatenate([both[:rows, :HDIM], both[rows:, HDIM:]], axis=0) / denom
        level = jnp.broadcast_to(top + jnp.log(denom), (2 * rows, HDIM))
        for entry in range(2):
            part = slice(entry * rows, (entry + 1) * rows)
            mean = summed[part].reshape(source_count, 8, HDIM)
            own = level[part].reshape(source_count, 8, HDIM)
            own = jnp.sum(jnp.where(lane % 8 == in_tile, own, 0.0), axis=1, keepdims=True)
            high = own.astype(BF16).astype(F32)
            middle = (own - high).astype(BF16).astype(F32)
            low = own - high - middle
            terms = jnp.where(lane < 8, high, jnp.where(lane < 16, middle, low))
            parts.append(jnp.where(in_tile == 6, terms, mean))
    return jnp.concatenate(parts, axis=1).astype(BF16)


def row_levels(values):
    source_count, message_rows, _ = values.shape
    tiles = values.reshape(source_count * message_rows // 8, 8, HDIM)
    in_tile = lax.broadcasted_iota(jnp.int32, tiles.shape, 1)
    lane = lax.broadcasted_iota(jnp.int32, tiles.shape, 2)
    terms = jnp.broadcast_to(tiles[:, 6:7, :], tiles.shape)
    picked = jnp.where((lane < 24) & (lane % 8 == in_tile), terms, 0.0)
    levels = jnp.sum(picked, axis=2, keepdims=True)
    return jnp.broadcast_to(levels, tiles.shape).reshape(values.shape)


def main_kernel(
    shard_ref, slot_ref, position_ref, length_ref,
    cross_ref, query_ref, fresh_ref, cache_ref, corpus_ref, weight_ref,
    self_ref, out_ref,
    shards, slots, cross, query, fresh, query_rows, fresh_rows, steps, columns, ranks, packed,
    cached, blocks, send, arrived, reply, returned, sums, levels,
    heads, gathered, weights, left, totals, out_send, out_recv,
    entered, local_sem, query_send, query_recv, reply_send, reply_recv,
    x_send, x_recv, ring_send, ring_recv, head_send, head_recv,
    y_send, y_recv, core_send, core_recv, out_send_sem, out_recv_sem,
):
    shard_count, message_rows, _ = send.shape
    x_count, y_count = GRID_OF[shard_count]
    layer = y_count * CORES
    tensor_count = heads.shape[0]
    request_count, step_count, _ = cross.shape
    me, mine = lax.axis_index("corpus"), lax.axis_index("tensor")
    x = me // layer
    y = (me // CORES) % y_count
    core = me % CORES
    turn = (x + mine) % 2

    def device_at(dx, dy, dc):
        return (((x + dx) % x_count) * y_count + (y + dy) % y_count) * CORES + (core + dc) % CORES

    def remote(source, target, send_sem, recv_sem, corpus=None, tensor=None):
        return pltpu.make_async_remote_copy(
            src_ref=source,
            dst_ref=target,
            send_sem=send_sem,
            recv_sem=recv_sem,
            device_id=(me if corpus is None else corpus, mine if tensor is None else tensor),
            device_id_type=MESH,
        )

    def far_first_of(count, step):
        return count // 2 + (1 - 2 * (step % 2)) * ((step + 1) // 2)

    def wait_bytes(ref, sem):
        pltpu.make_async_copy(ref, ref, sem).wait()

    small = [
        pltpu.make_async_copy(source, target, local_sem.at[index])
        for index, (source, target) in enumerate(
            [(shard_ref, shards), (slot_ref, slots), (cross_ref, cross), (query_ref, query),
             (fresh_ref, fresh)]
        )
    ]
    for copy in small:
        copy.start()

    barrier = pltpu.get_barrier_semaphore()

    def greet(sem, corpus, tensor):
        pl.semaphore_signal(sem, inc=1, device_id=(corpus, tensor), device_id_type=MESH)

    for dx in range(1, x_count):
        greet(barrier, device_at(dx, 0, 0), mine)

    def greet_layer(step, carry):
        greet(barrier, device_at(0, step // CORES, step % CORES), mine)
        return carry

    def greet_tensor(step, carry):
        greet(barrier, me, (mine + step) % tensor_count)
        return carry

    lax.fori_loop(1, layer, greet_layer, 0)
    lax.fori_loop(1, tensor_count, greet_tensor, 0)
    own_place = weights.at[mine // 2, x]
    own_weight = pltpu.make_async_copy(weight_ref, own_place, local_sem.at[5])
    pl.when(turn == 0)(own_weight.start)
    cache_copy = pltpu.make_async_copy(cache_ref, cached, local_sem.at[6])
    corpus_copy = pltpu.make_async_copy(corpus_ref, blocks, local_sem.at[7])
    cache_copy.start()
    corpus_copy.start()
    pl.semaphore_wait(barrier, x_count - 1 + layer - 1 + tensor_count - 1)
    for dx in range(1, x_count):
        greet(entered, device_at(dx, 0, 0), mine)

    def send_weight(dx):
        remote(
            weight_ref, weights.at[mine // 2, x], x_send, x_recv.at[dx], device_at(dx, 0, 0)
        ).start()

    odd_steps, even_steps = range(1, x_count, 2), range(2, x_count, 2)

    @pl.when(turn == 1)
    def _():
        for dx in odd_steps:
            send_weight(dx)

    @pl.when(turn == 0)
    def _():
        for dx in even_steps:
            send_weight(dx)

    last_step, half_count = tensor_count // 2 - 1, x_count // 2

    def ring_copy(down, step, offset):
        owner = (mine + (step if down else tensor_count - step)) % tensor_count
        piece = weights.at[owner // 2, (x + offset) % x_count]
        after = (mine + (tensor_count - 1 if down else 1)) % tensor_count
        return remote(
            piece, piece, ring_send.at[down, step, offset], ring_recv.at[down, step, offset],
            tensor=after,
        )

    def ring_ways(step, offset):
        if step == last_step:
            return (0,) if offset < half_count else (1,)
        return (0, 1) if 0 <= step < last_step else ()

    def ring_wait(step, offset):
        for down in ring_ways(step, offset):
            ring_copy(down, step, offset).wait_recv()

    def ring_step(step, offset):
        if step > last_step:
            return

        @pl.when((turn + step) % 2 == 0)
        def _():
            ring_wait(step - 1, offset)
            for down in ring_ways(step, offset):
                ring_copy(down, step, offset).start()

    pl.when(turn == 0)(own_weight.wait)
    ring_step(0, 0)
    for copy in small:
        copy.wait()
    pack_queries(shards, slots, cross, steps, columns, ranks, packed, send)
    own_query = pltpu.make_async_copy(send.at[me], arrived.at[me], query_recv.at[0])
    own_query.start()
    ring_step(1, 0)

    def both_cores(dx, dy):
        row = (((x + dx) % x_count) * y_count + (y + dy) % y_count) * CORES
        return row + core, row + 1 - core

    def send_query(target, dx):
        remote(send.at[target], arrived.at[me], query_send, query_recv.at[dx], target).start()

    def send_queries(dx, first):
        def body(dy, carry):
            for target in both_cores(dx, far_first_of(y_count, dy)):
                send_query(target, dx)
            return carry

        if first:
            send_query(both_cores(0, 0)[1], 0)
        lax.fori_loop(0, y_count - first, body, 0)

    send_queries(0, 1)
    pl.semaphore_wait(entered, x_count - 1)
    for dx in range(1, x_count):
        send_queries(dx, 0)

    for request in range(request_count):
        rows = slice(request * step_count, (request + 1) * step_count)
        query_rows[rows, :] = query[request].astype(F32)
        for index in range(2):
            fresh_rows[index, rows, :] = fresh[request, index].astype(F32)
    cache_copy.wait()
    all_heads = range(message_rows // 8)

    for offset in range(1, x_count):
        @pl.when(turn == 0)
        def _():
            source = weights.at[mine // 2, (x + offset) % x_count]
            wait_bytes(source, x_recv.at[x_count - offset])

        ring_step(0, offset)
    attend_self(query_rows, fresh_rows, cached, length_ref, self_ref, all_heads[:2])
    ring_step(2, 0)
    attend_self(query_rows, fresh_rows, cached, length_ref, self_ref, all_heads[2:])
    corpus_copy.wait()

    def serve(dx, carry):
        first = pl.multiple_of(((x - dx + x_count) % x_count) * layer, layer)
        chunk = pl.ds(first, layer)
        wait_bytes(arrived.at[chunk], query_recv.at[dx])
        reply[chunk] = attend_blocks(arrived[chunk], blocks)

        def send_reply(target):
            remote(
                reply.at[target], returned.at[me], reply_send, reply_recv.at[dx], target
            ).start()

        def answer(dy, inner):
            for target in both_cores(x_count - dx, far_first_of(y_count, dy)):
                send_reply(target)
            return inner

        pl.when(dx == 0)(lambda: send_reply(both_cores(0, 0)[1]))
        lax.fori_loop(0, y_count - jnp.where(dx == 0, 1, 0), answer, 0)
        if last_step > 0:
            for index, (step, offset) in enumerate(((1, 1), (1, 2), (1, 3), (2, 1))):
                pl.when(dx == index)(functools.partial(ring_step, step, offset))
        return carry

    lax.fori_loop(0, x_count, serve, 0)
    own_reply = pltpu.make_async_copy(reply.at[me], returned.at[me], reply_recv.at[0])
    own_reply.start()
    ring_step(2, 2)

    def decode(dx, carry):
        first = pl.multiple_of(((x + dx) % x_count) * layer, layer)
        chunk = pl.ds(first, layer)
        wait_bytes(returned.at[chunk], reply_recv.at[dx])
        values = returned[chunk].astype(F32)
        sums[chunk] = values
        levels[chunk] = row_levels(values)
        if last_step > 1:
            for index, (step, offset) in ((0, (2, 3)),):
                pl.when(dx == index)(functools.partial(ring_step, step, offset))
        return carry

    lax.fori_loop(0, x_count, decode, 0)

    tile_row = lax.broadcasted_iota(jnp.int32, (message_rows, HDIM), 0) % 8

    def combined(request):
        boundary = SPAN - position_ref[request] % SPAN
        late = tile_row >= boundary

        def item(ref, number):
            tile = ref[shards[number, request]]
            second = ranks[pl.ds(number * request_count + request, 1), :] == 1.0
            if number < NBR:
                return jnp.where(second, pltpu.roll(tile, message_rows - 3, 0), tile)
            return jnp.where(
                second, pltpu.roll(tile, message_rows - 2, 0), pltpu.roll(tile, 1, 0)
            )

        def pair(ref):
            return [
                jnp.where(late, item(ref, NBR + number), item(ref, number)) for number in range(NBR)
            ]

        held, level = pair(sums), pair(levels)
        joint = jnp.maximum(level[0], level[1])
        factors = [jnp.exp(entry - joint) for entry in level]
        return (factors[0] * held[0] + factors[1] * held[1]) / (factors[0] + factors[1])

    def combine(owner):
        first = combined(owner * 2)
        second = pltpu.roll(combined(owner * 2 + 1), 4, 0)
        both = jnp.where(tile_row < 4, first, second)
        upper = jnp.concatenate([both[0:8], both[8:16]], axis=1)
        lower = jnp.concatenate([both[16:24], both[24:32]], axis=1)
        heads[owner] = jnp.concatenate([upper, lower], axis=0).astype(BF16)


    place = y * CORES + core
    taker = device_at(jnp.where(x % 2 == 0, turn, x_count - turn), 0, 0)

    def head_copy(owner):
        return remote(
            heads.at[owner], gathered.at[place, x % 2, mine // 2], head_send, head_recv,
            taker, owner,
        )

    own_heads = pltpu.make_async_copy(
        heads.at[mine], gathered.at[place, x % 2, mine // 2], head_recv
    )

    def send_heads(step, carry):
        owner = (mine + far_first_of(tensor_count, step)) % tensor_count
        combine(owner)
        head_copy(owner).start()
        return carry

    lax.fori_loop(0, tensor_count - 1, send_heads, 0)
    combine(mine)
    pl.when(turn == 0)(own_heads.start)

    @pl.when(turn == 1)
    def _():
        head_copy(mine).start()

    wait_bytes(gathered.at[place], head_recv)

    def slot_at(dy):
        return ((y + dy) % y_count) * CORES + core

    def send_y(ref, dy, number):
        return remote(ref, ref, y_send.at[number], y_recv.at[number], device_at(0, dy, 0))

    def pass_core(index):
        remote(
            gathered.at[index], gathered.at[index], core_send, core_recv, device_at(0, 0, 1)
        ).start()

    own = gathered.at[place]
    if y_count == 8:
        up, down = 1, y_count - 1

        def half_of(index, number):
            return gathered.at[index, pl.ds(number, 1)]

        y_copies = []

        def start_y(ref, dy, number):
            copy = send_y(ref, dy, number)
            copy.start()
            y_copies.append(copy)

        for number in range(2):
            start_y(half_of(place, number), 2, 2 + number)
            start_y(half_of(place, 1 - number), y_count - 2, 5 - number)
        start_y(own, up, 0)
        start_y(own, down, 1)
        pass_core(place)
        for offset in range(x_count):
            ring_step(3, offset)
        below, above = slot_at(y_count - 2), slot_at(2)
        for number in range(2):
            low_half, high_half = half_of(below, number), half_of(above, 1 - number)
            wait_bytes(low_half, y_recv.at[2 + number])
            if number == 0:
                start_y(low_half, 2, 10)
            start_y(low_half, up, 6 + number)
            wait_bytes(high_half, y_recv.at[5 - number])
            if number == 0:
                start_y(high_half, y_count - 2, 11)
            start_y(high_half, down, 9 - number)
        pass_core(below)
        pass_core(above)
        for dy, number in ((down, 0), (up, 1)):
            wait_bytes(gathered.at[slot_at(dy)], y_recv.at[number])
            pass_core(slot_at(dy))
        for dy, number in ((y_count - 3, 6), (3, 8)):
            for part in range(2):
                wait_bytes(half_of(slot_at(dy), part), y_recv.at[number + part])
            pass_core(slot_at(dy))
        wait_bytes(half_of(slot_at(4), 0), y_recv.at[10])
        wait_bytes(half_of(slot_at(4), 1), y_recv.at[11])
        pass_core(slot_at(4))
    else:
        y_copies = [send_y(own, dy, dy) for dy in range(1, y_count)]
        for copy in y_copies:
            copy.start()
        pass_core(place)
        for dy in range(1, y_count):
            wait_bytes(gathered.at[slot_at(y_count - dy)], y_recv.at[dy])
            pass_core(slot_at(y_count - dy))

    @pl.when((turn + last_step + 1) % 2 == 0)
    def _():
        for offset in range(x_count):
            ring_wait(last_step, offset)

    wait_bytes(gathered.at[pl.ds(0, y_count)], core_recv)

    half = gathered.shape[3] // 2
    rows = layer * 2 * half

    features = weights.shape[2]
    for owner in range(tensor_count // 2):
        block = gathered[:, :, owner].astype(F32)
        left[:, owner * features : (owner + 1) * features] = jnp.concatenate(
            [block[:, :, :half].reshape(rows, -1), block[:, :, half:].reshape(rows, -1)], axis=1
        ).astype(BF16)

    def send_out(dx):
        target = (x + dx) % x_count
        if dx == 0:
            pltpu.make_async_copy(out_send.at[x], out_recv.at[x], out_recv_sem).start()
        else:
            remote(
                out_send.at[target], out_recv.at[x], out_send_sem, out_recv_sem,
                device_at(dx, 0, 0),
            ).start()

    far_first = sorted(range(x_count), key=lambda dx: -min(dx, x_count - dx))
    for first in range(0, x_count, 2):
        group = far_first[first : first + 2]
        product = None
        for owner in range(tensor_count // 2):
            right = jnp.concatenate(
                [weights[owner, (x + dx) % x_count] for dx in group], axis=1
            )
            term = jnp.dot(
                left[:, owner * features : (owner + 1) * features], right,
                preferred_element_type=F32,
            )
            product = term if product is None else product + term
        for index, dx in enumerate(group):
            totals[...] = product[:, index * HDIM : (index + 1) * HDIM]
            for column in range(2):
                for row in range(half):
                    picked = totals[pl.ds(column * half + row, layer, stride=2 * half), :]
                    out_send[(x + dx) % x_count, column, row] = picked.astype(BF16)
            send_out(dx)
    wait_bytes(out_recv, out_recv_sem)
    for index in range(x_count):
        pair, column = index // 2 * 2, index % 2
        both = out_recv[pair, column].astype(F32) + out_recv[pair + 1, column].astype(F32)
        out_ref[:, index * layer : (index + 1) * layer, :] = both.astype(BF16)

    wait_bytes(send.at[pl.ds(0, shard_count - 1)], query_send)
    wait_bytes(reply.at[pl.ds(0, shard_count - 1)], reply_send)
    for way, steps_sent in ((1, odd_steps), (0, even_steps)):
        if len(steps_sent):
            sent = weights.at[0, pl.ds(0, len(steps_sent))]
            pl.when(turn == way)(functools.partial(wait_bytes, sent, x_send))
    for step in range(last_step + 1):
        @pl.when((turn + step) % 2 == 0)
        def _():
            for offset in range(x_count):
                for down in ring_ways(step, offset):
                    ring_copy(down, step, offset).wait_send()
    wait_bytes(heads.at[pl.ds(0, tensor_count - 1)], head_send)
    pl.when(turn == 1)(functools.partial(wait_bytes, heads.at[0], head_send))
    for copy in y_copies:
        copy.wait_send()
    wait_bytes(gathered.at[pl.ds(0, y_count)], core_send)
    wait_bytes(out_send.at[pl.ds(0, x_count - 1)], out_send_sem)


def hand_on_kernel(self_in, out_in, self_out, out_out, sems):
    copies = [
        pltpu.make_async_copy(self_in, self_out, sems.at[0]),
        pltpu.make_async_copy(out_in, out_out, sems.at[1]),
    ]
    for copy in copies:
        copy.start()
    for copy in copies:
        copy.wait()


def on_device(
    self_query,
    cross_query,
    cache,
    step_kv,
    kv_length,
    positions,
    corpus_kv,
    neighbour_shard,
    neighbour_slot,
    out_weight,
):
    request_count, step_count, width = cross_query.shape
    head_count = width // HDIM
    shard_count = lax.axis_size("corpus")
    tensor_count = lax.axis_size("tensor")
    x_count, y_count = GRID_OF[shard_count]
    layer = y_count * CORES
    message_rows = head_count * 8
    row_count = request_count * step_count
    share = row_count // tensor_count
    smem = pl.BlockSpec(memory_space=pltpu.SMEM)
    vmem = pl.BlockSpec(memory_space=pltpu.VMEM)
    hbm = pl.BlockSpec(memory_space=pl.ANY)
    message = (shard_count, message_rows, HDIM)
    gather_shape = (layer, 2, tensor_count // 2, 2 * share, width // 2)
    out_shape = (share, shard_count, out_weight.shape[1])
    exchange = (x_count, 2, share, layer, out_weight.shape[1])
    dma = pltpu.SemaphoreType.DMA
    ring_shape = (2, max(1, tensor_count // 2), x_count)
    self_heads, cross_out = pl.pallas_call(
        main_kernel,
        out_shape=(
            jax.ShapeDtypeStruct(self_query.shape, BF16),
            jax.ShapeDtypeStruct(out_shape, BF16),
        ),
        in_specs=[hbm] * 2 + [smem] * 2 + [hbm] * 6,
        out_specs=(vmem, vmem),
        scratch_shapes=[
            pltpu.SMEM((2 * NBR, request_count), jnp.int32),
            pltpu.SMEM((2 * NBR, request_count), jnp.int32),
            pltpu.VMEM(cross_query.shape, BF16),
            pltpu.VMEM(self_query.shape, BF16),
            pltpu.VMEM(step_kv.shape, BF16),
            pltpu.VMEM((row_count, width), F32),
            pltpu.VMEM((2, row_count, width), F32),
            pltpu.VMEM((step_count, request_count, width), F32),
            pltpu.VMEM((2 * NBR * request_count, HDIM), jnp.int32),
            pltpu.VMEM((2 * NBR * request_count, HDIM), F32),
            pltpu.VMEM((shard_count * message_rows, HDIM), F32),
            pltpu.VMEM(cache.shape, BF16),
            pltpu.VMEM(corpus_kv.shape, BF16),
            pltpu.VMEM(message, BF16),
            pltpu.VMEM(message, BF16),
            pltpu.VMEM(message, BF16),
            pltpu.VMEM(message, BF16),
            pltpu.VMEM(message, F32),
            pltpu.VMEM(message, F32),
            pltpu.VMEM((tensor_count, 2 * share, width // 2), BF16),
            pltpu.VMEM(gather_shape, BF16),
            pltpu.VMEM((tensor_count // 2, x_count, width, HDIM), BF16),
            pltpu.VMEM((layer * 2 * share, tensor_count // 2 * width), BF16),
            pltpu.VMEM((layer * 2 * share, HDIM), F32),
            pltpu.VMEM(exchange, BF16),
            pltpu.VMEM(exchange, BF16),
            pltpu.SemaphoreType.REGULAR,
            dma((8,)),
            dma, dma((x_count,)),
            dma, dma((x_count,)),
            dma, dma((x_count,)),
            dma(ring_shape), dma(ring_shape),
            dma, dma,
            dma((12,)), dma((12,)),
            dma, dma,
            dma, dma,
        ],
        compiler_params=pltpu.CompilerParams(
            collective_id=0, has_side_effects=True, vmem_limit_bytes=56 * 1024 * 1024
        ),
        name="retrieve_and_project",
    )(
        neighbour_shard.T, neighbour_slot.T, positions, kv_length,
        cross_query, self_query, step_kv, cache, corpus_kv, out_weight,
    )
    return pl.pallas_call(
        hand_on_kernel,
        out_shape=(
            jax.ShapeDtypeStruct(self_query.shape, BF16),
            jax.ShapeDtypeStruct(out_shape, BF16),
        ),
        in_specs=[vmem] * 2,
        out_specs=(hbm, hbm),
        scratch_shapes=[dma((2,))],
        name="hand_on",
    )(self_heads, cross_out)


def solution(mesh):
    return jax.shard_map(
        on_device,
        mesh=mesh,
        in_specs=(
            P("corpus", None, "tensor"),
            P("corpus", None, "tensor"),
            P("corpus", None, None, "tensor"),
            P("corpus", None, None, "tensor"),
            P("corpus"),
            P("corpus"),
            P("corpus", None, None, "tensor"),
            P("corpus", None),
            P("corpus", None),
            P("tensor", "corpus"),
        ),
        out_specs=(P("corpus", None, "tensor"), P("tensor", None, "corpus")),
        check_vma=False,
    )
```
